256 devices in a mesh: dp: 8 (over x, y_hi), tensor: 32 (over z, y_lo, core).
Axes of the slice: x: 4, y: 4 (y_hi: 2, y_lo: 2; y = y_hi * 2 + y_lo), z: 8, core: 2. Of those that a mesh axis runs over, the one named last changes fastest.
Arguments:
- projection_input: bfloat16 [2048, 8192], P('dp', 'tensor'), may hold values from -6 to 6
- output_gradient: bfloat16 [2048, 8192], P('dp', 'tensor'), may hold values from -6 to 6
- adapter_down: float32 [8192, 64], P('tensor'), may hold values from -0.0625 to 0.0625
- adapter_up: float32 [64, 8192], P(None, 'tensor'), may hold values from -0.75 to 0.75
- down_first_moment: float32 [8192, 64], P('tensor'), may hold values from -4 to 4
- down_second_moment: float32 [8192, 64], P('tensor'), may hold values from 0.01 to 1
- up_first_moment: float32 [64, 8192], P(None, 'tensor'), may hold values from -0.4375 to 0.4375
- up_second_moment: float32 [64, 8192], P(None, 'tensor'), may hold values from 0.0001 to 0.01
- projection_weight: bfloat16 [8192, 8192], P('tensor'), may hold values from -0.0625 to 0.0625
- queries: bfloat16 [4, 512, 8192], P(None, 'dp', 'tensor')
- stored_keys: bfloat16 [512, 128, 4096], P('dp', None, 'tensor'), as said below
- stored_values: bfloat16 [512, 128, 4096], P('dp', None, 'tensor'), as said below
- fresh_keys: bfloat16 [4, 512, 4096], P(None, 'dp', 'tensor'), as said below
- fresh_values: bfloat16 [4, 512, 4096], P(None, 'dp', 'tensor'), as said below
- lengths: int32 [512], P('dp'), may hold values from 1 to 128, as said below
Outputs:
- decoded: bfloat16 [4, 512, 8192], P(None, 'dp', 'tensor')
- stepped_down: float32 [8192, 64], P('tensor')
- stepped_up: float32 [64, 8192], P(None, 'tensor')
- stepped_down_first: float32 [8192, 64], P('tensor')
- stepped_down_second: float32 [8192, 64], P('tensor')
- stepped_up_first: float32 [64, 8192], P(None, 'tensor')
- stepped_up_second: float32 [64, 8192], P(None, 'tensor')
The draws below stay inside these ranges and needn't reach their ends.
Inputs may be any that keep to these rules, and one draw needn't show every extreme that they name: `lengths`: the largest length is 128 in every draw. `stored_keys`: 8 key heads of size 128; features t * 128 to (t+1) * 128 - 1 hold head t // (32 / 8), so each head stands at 32 / 8 neighbouring tensor indices. `stored_values`: 8 value heads, laid out as stored_keys. `fresh_keys`: 8 key heads, laid out as stored_keys. `fresh_values`: 8 value heads, laid out as stored_keys.
All inputs are finite; a program needn't handle non-finite values.
Results may differ from the reference program's by a relative error of at most 0.0057.
Values sent between devices are 32-bit elements; how exact they have to be, the bound alone decides.
A program may use at most 64 MiB of HBM per device.

```python
import math
import jax
import jax.numpy as jnp
from jax import lax

MODEL_WIDTH = 8192
HQ = 64
HD = 128
KVH = 8
ADAPTER_RANK = 64
STEPS = 4
CACHE = 128
TRAIN_TOKENS = 2048
ROLL = 512
N_TENSOR = 32


def shared_heads(key, lead):
    drawn = jax.random.normal(key, lead + (KVH, 1, HD), jnp.float32)
    drawn = jnp.clip(drawn, -6.0, 6.0)
    copies = jnp.broadcast_to(drawn, lead + (KVH, N_TENSOR // KVH, HD))
    return copies.reshape(lead + (N_TENSOR * HD,)).astype(jnp.bfloat16)


def draw_queries(key, part):
    key = jax.random.fold_in(key, 5)
    entries = jax.random.normal(key, (STEPS, ROLL, MODEL_WIDTH), jnp.float32)
    return entries.astype(jnp.bfloat16)


def draw_stored_keys(key, part):
    key = jax.random.fold_in(key, 11)
    return shared_heads(key, (ROLL, CACHE))


def draw_stored_values(key, part):
    key = jax.random.fold_in(key, 13)
    return shared_heads(key, (ROLL, CACHE))


def draw_fresh_keys(key, part):
    key = jax.random.fold_in(key, 17)
    return shared_heads(key, (STEPS, ROLL))


def draw_fresh_values(key, part):
    key = jax.random.fold_in(key, 19)
    return shared_heads(key, (STEPS, ROLL))


def draw_lengths(key, part):
    key = jax.random.fold_in(key, 7)
    drawn = jax.random.randint(key, (ROLL,), 1, CACHE + 1)
    chosen = jax.random.randint(jax.random.fold_in(key, 1), (), 0, ROLL)
    return drawn.at[chosen].set(CACHE).astype(jnp.int32)


def block_scale(stream_key, extent, pieces, low, high):
    loudness = 1.0
    for position, shards_of in pieces:
        draws = jax.random.uniform(jax.random.fold_in(jax.random.fold_in(stream_key, 6), position), (shards_of,), jnp.float32, low / len(pieces), high / len(pieces))
        loudness = loudness * jnp.repeat(jnp.exp(draws), extent[position] // shards_of).reshape((-1,) + (1,) * (len(extent) - 1 - position))
    return loudness


def scatter_about(own_key, shape, spread, reach, pieces=(), held_as=jnp.bfloat16):
    array = jax.random.normal(own_key, shape, jnp.float32) * spread
    if len(pieces) > 0:
        array = block_scale(own_key, shape, pieces, -0.22, 0.18) * array
    return jnp.clip(array, min=-reach, max=reach).astype(held_as)


def setup_inputs(seed: int = 0) -> dict:
    key_of = jax.random.split(jax.random.key(seed), 16)
    projection_input = scatter_about(key_of[0], (TRAIN_TOKENS, MODEL_WIDTH), 1.0, 6.0, ((0, 8), (1, 32)))
    output_gradient = scatter_about(key_of[1], (TRAIN_TOKENS, MODEL_WIDTH), 1.0, 6.0, ((0, 8), (1, 32)))
    adapter_down = scatter_about(key_of[2], (MODEL_WIDTH, ADAPTER_RANK), MODEL_WIDTH ** -0.5, 0.0625, ((0, 32),), jnp.float32)
    adapter_up = scatter_about(key_of[3], (ADAPTER_RANK, MODEL_WIDTH), ADAPTER_RANK ** -0.5, 0.75, ((1, 32),), jnp.float32)
    down_first_moment = scatter_about(key_of[4], (MODEL_WIDTH, ADAPTER_RANK), 0.3, 4.0, ((0, 32),), jnp.float32)
    down_second_moment = jnp.clip(jnp.exp(math.log(1.0) - 4.6051702 * jax.random.uniform(key_of[5], (MODEL_WIDTH, ADAPTER_RANK), jnp.float32) ** block_scale(key_of[5], (MODEL_WIDTH, ADAPTER_RANK), ((0, 32),), -0.2, 0.2)), 0.01, 1.0)
    up_first_moment = scatter_about(key_of[6], (ADAPTER_RANK, MODEL_WIDTH), 0.03, 0.4375, ((1, 32),), jnp.float32)
    up_second_moment = jnp.clip(jnp.exp(math.log(0.01) - 4.6051702 * jax.random.uniform(key_of[7], (ADAPTER_RANK, MODEL_WIDTH), jnp.float32) ** block_scale(key_of[7], (ADAPTER_RANK, MODEL_WIDTH), ((1, 32),), -0.2, 0.2)), 0.0001, 0.01)
    projection_weight = scatter_about(key_of[8], (MODEL_WIDTH, MODEL_WIDTH), MODEL_WIDTH ** -0.5, 0.0625, ((0, 32),))
    queries = draw_queries(jax.random.fold_in(key_of[15], 71), 0)
    stored_keys = draw_stored_keys(jax.random.fold_in(key_of[15], 71), 0)
    stored_values = draw_stored_values(jax.random.fold_in(key_of[15], 71), 0)
    fresh_keys = draw_fresh_keys(jax.random.fold_in(key_of[15], 71), 0)
    fresh_values = draw_fresh_values(jax.random.fold_in(key_of[15], 71), 0)
    lengths = draw_lengths(jax.random.fold_in(key_of[15], 71), 0)
    return dict(projection_input=projection_input, output_gradient=output_gradient, adapter_down=adapter_down, adapter_up=adapter_up, down_first_moment=down_first_moment, down_second_moment=down_second_moment, up_first_moment=up_first_moment, up_second_moment=up_second_moment, projection_weight=projection_weight, queries=queries, stored_keys=stored_keys, stored_values=stored_values, fresh_keys=fresh_keys, fresh_values=fresh_values, lengths=lengths)


beta_one = 0.9
beta_two = 0.999
learn_rate = 0.005
adam_count = 10.0
adam_eps = 1e-08
adapter_scale = 2.0

def apply_adam_step(current, moment_one, moment_two, gradient):
    moment_one = beta_one * moment_one + (1.0 - beta_one) * gradient
    moment_two = beta_two * moment_two + (1.0 - beta_two) * gradient * gradient
    fix_one = 1.0 - beta_one ** adam_count
    fix_two = 1.0 - beta_two ** adam_count
    updated = current - learn_rate * (moment_one / fix_one) / (jnp.sqrt(moment_two / fix_two) + adam_eps)
    return (updated, moment_one, moment_two)

def reference(projection_input, output_gradient, adapter_down, adapter_up, down_first_moment, down_second_moment, up_first_moment, up_second_moment, projection_weight, queries, stored_keys, stored_values, fresh_keys, fresh_values, lengths):
    highest_precision = lax.Precision.HIGHEST
    input_wide_float = projection_input.astype(jnp.float32)
    gradient_wide_float = output_gradient.astype(jnp.float32)
    input_times_down = jnp.dot(input_wide_float, adapter_down, precision=highest_precision)
    gradient_through_up = jnp.dot(gradient_wide_float, adapter_up.T, precision=highest_precision)
    scale_coefficient = adapter_scale / TRAIN_TOKENS
    down_gradient = scale_coefficient * jnp.dot(input_wide_float.T, gradient_through_up, precision=highest_precision)
    up_gradient = scale_coefficient * jnp.dot(input_times_down.T, gradient_wide_float, precision=highest_precision)
    stepped_down, stepped_down_first, stepped_down_second = apply_adam_step(adapter_down, down_first_moment, down_second_moment, down_gradient)
    stepped_up, stepped_up_first, stepped_up_second = apply_adam_step(adapter_up, up_first_moment, up_second_moment, up_gradient)
    group_size = HQ // N_TENSOR
    inv_root = 1.0 / math.sqrt(HD)
    query_heads = queries.astype(jnp.float32).reshape(STEPS, ROLL, N_TENSOR, group_size, HD)
    keys_cache = stored_keys.astype(jnp.float32).reshape(ROLL, CACHE, N_TENSOR, HD)
    values_cache = stored_values.astype(jnp.float32).reshape(ROLL, CACHE, N_TENSOR, HD)
    keys_new = fresh_keys.astype(jnp.float32).reshape(STEPS, ROLL, N_TENSOR, HD)
    values_new = fresh_values.astype(jnp.float32).reshape(STEPS, ROLL, N_TENSOR, HD)
    score_cache = jnp.einsum('srkgd,rckd->srkgc', query_heads, keys_cache) * inv_root
    score_new = jnp.einsum('srkgd,jrkd->srkgj', query_heads, keys_new) * inv_root
    cache_live = (jnp.arange(CACHE)[None, :] < lengths[:, None])[None, :, None, None, :]
    new_live = (jnp.arange(STEPS)[None, :] <= jnp.arange(STEPS)[:, None])[:, None, None, None, :]
    score_cache = jnp.where(cache_live, score_cache, -1e+30)
    score_new = jnp.where(new_live, score_new, -1e+30)
    largest = jnp.maximum(lax.optimization_barrier(jnp.max(score_cache, axis=-1)), lax.optimization_barrier(jnp.max(score_new, axis=-1)))[..., None]
    exp_cache = jnp.where(cache_live, jnp.exp(score_cache - largest), 0.0)
    exp_new = jnp.where(new_live, jnp.exp(score_new - largest), 0.0)
    total = (lax.optimization_barrier(jnp.sum(exp_cache, axis=-1)) + lax.optimization_barrier(jnp.sum(exp_new, axis=-1)))[..., None]
    weight_cache = (exp_cache / total).astype(jnp.bfloat16).astype(jnp.float32)
    weight_new = (exp_new / total).astype(jnp.bfloat16).astype(jnp.float32)
    mixed = jnp.einsum('srkgc,rckd->srkgd', weight_cache, values_cache)
    mixed = mixed + jnp.einsum('srkgj,jrkd->srkgd', weight_new, values_new)
    attention_output = mixed.reshape(STEPS * ROLL, MODEL_WIDTH).astype(jnp.bfloat16)
    base = jnp.dot(attention_output, projection_weight, preferred_element_type=jnp.float32)
    adapter_row_count = jnp.dot(attention_output.astype(jnp.float32), stepped_down, precision=highest_precision)
    adapter_delta = adapter_scale * jnp.dot(adapter_row_count, stepped_up, precision=highest_precision)
    decoded = (base + adapter_delta).reshape(STEPS, ROLL, MODEL_WIDTH).astype(jnp.bfloat16)
    return (decoded, stepped_down, stepped_up, stepped_down_first, stepped_down_second, stepped_up_first, stepped_up_second)
```

```python
import functools
import math

import jax
import jax.numpy as jnp
from jax import lax
from jax.experimental import pallas as pl
from jax.experimental.pallas import tpu as pltpu
from jax.sharding import PartitionSpec as P

beta_one = 0.9
beta_two = 0.999
learn_rate = 0.005
adam_count = 10.0
adam_eps = 1e-08
adapter_scale = 2.0

F32 = jnp.float32
BF16 = jnp.bfloat16
MESH = pl.DeviceIdType.MESH

ROWS = 256
FEAT = 256
RANK = 64
ZN = 8
DP = 8
HALF = ROWS // 2
ROWS_A = 64
ROWS_B = HALF - ROWS_A


def apply_adam_step(current, moment_one, moment_two, gradient):
    moment_one = beta_one * moment_one + (1.0 - beta_one) * gradient
    moment_two = beta_two * moment_two + (1.0 - beta_two) * gradient * gradient
    fix_one = 1.0 - beta_one**adam_count
    fix_two = 1.0 - beta_two**adam_count
    updated = current - learn_rate * (moment_one / fix_one) / (
        jnp.sqrt(moment_two / fix_two) + adam_eps
    )
    return (updated, moment_one, moment_two)


def dot(a, b):
    return jnp.dot(a, b, preferred_element_type=F32)


def dot_t(a, b):
    return lax.dot_general(a, b, (((1,), (1,)), ((), ())), preferred_element_type=F32)


def two_terms(a):
    high = a.astype(BF16)
    low = (a - high.astype(F32)).astype(BF16)
    return high, low


def attention_kernel(
    len_ref, q_ref, k_ref, v_ref, fk_ref, fv_ref, out_ref, qs, sc, sn, wc, mixed
):
    pairs = k_ref.shape[0] // 2
    inv_root = 1.0 / math.sqrt(128)
    i0 = lax.broadcasted_iota(jnp.int32, (ROWS, ROWS), 0)
    i1 = lax.broadcasted_iota(jnp.int32, (ROWS, ROWS), 1)
    perm = jnp.where(i1 == (i0 % 4) * 64 + i0 // 4, 1.0, 0.0).astype(BF16)
    qp = dot(perm, q_ref[...])
    qp = jnp.concatenate(
        [qp[:, :128].reshape(pairs, 8, 128), qp[:, 128:].reshape(pairs, 8, 128)], axis=1
    )
    qs[...] = qp.reshape(pairs * 16, 128).astype(BF16)
    fk = dot(perm, fk_ref[...]).astype(BF16)
    fv = dot(perm, fv_ref[...]).astype(BF16)

    row = lax.broadcasted_iota(jnp.int32, (16, 256), 0)
    col = lax.broadcasted_iota(jnp.int32, (16, 256), 1)
    second = (row // 4) % 2 == 1

    def scores(p, carry):
        keys = k_ref[pl.ds(2 * p, 2)].reshape(256, 128)
        at = pl.ds(pl.multiple_of(p * 16, 16), 16)
        s = dot_t(qs[at, :], keys) * inv_root
        start = jnp.where(second, 128, 0)
        stop = jnp.where(second, 128 + len_ref[2 * p + 1], len_ref[2 * p])
        sc[at, :] = jnp.where((col >= start) & (col < stop), s, -jnp.inf)
        return carry

    lax.fori_loop(0, pairs, scores, 0, unroll=8)

    nrow = lax.broadcasted_iota(jnp.int32, (256, 128), 0)
    ncol = lax.broadcasted_iota(jnp.int32, (256, 128), 1)
    request = (nrow // 16) * 2 + (nrow // 4) % 2
    new_live = (ncol // 4 == request) & (ncol % 4 <= nrow % 4)
    for half in range(2):
        part = pl.ds(half * 256, 256)
        s = dot_t(qs[part, :], fk[half * 128 : half * 128 + 128]) * inv_root
        sn[part, :] = jnp.where(new_live, s, -jnp.inf)

    for block in range(8):
        part = pl.ds(block * 64, 64)
        s, n = sc[part, :], sn[part, :]
        largest = jnp.maximum(
            jnp.max(s, axis=1, keepdims=True), jnp.max(n, axis=1, keepdims=True)
        )
        e, m = jnp.exp(s - largest), jnp.exp(n - largest)
        total = jnp.sum(e, axis=1, keepdims=True) + jnp.sum(m, axis=1, keepdims=True)
        scale = 1.0 / total
        wc[part, :] = (e * scale).astype(BF16)
        where_new = (block // 4) * 128
        mixed[part, :] = dot((m * scale).astype(BF16), fv[where_new : where_new + 128])

    def mix(p, carry):
        values = v_ref[pl.ds(2 * p, 2)].reshape(256, 128)
        at = pl.ds(pl.multiple_of(p * 16, 16), 16)
        mixed[at, :] += dot(wc[at, :], values)
        return carry

    lax.fori_loop(0, pairs, mix, 0, unroll=8)
    o = mixed[...].reshape(pairs, 16, 128)
    out_ref[:, :128] = o[:, :8].reshape(ROWS, 128).astype(BF16)
    out_ref[:, 128:] = o[:, 8:].reshape(ROWS, 128).astype(BF16)


def attention(lengths, queries, keys, values, fresh_keys, fresh_values):
    vmem = pl.BlockSpec(memory_space=pltpu.VMEM)
    return pl.pallas_call(
        attention_kernel,
        out_shape=jax.ShapeDtypeStruct((ROWS, FEAT), BF16),
        in_specs=[pl.BlockSpec(memory_space=pltpu.SMEM)] + [vmem] * 5,
        out_specs=vmem,
        scratch_shapes=[
            pltpu.VMEM((512, 128), BF16),
            pltpu.VMEM((512, 256), F32),
            pltpu.VMEM((512, 128), F32),
            pltpu.VMEM((512, 256), BF16),
            pltpu.VMEM((512, 128), F32),
        ],
        compiler_params=pltpu.CompilerParams(vmem_limit_bytes=24 * 1024 * 1024),
    )(lengths, queries, keys, values, fresh_keys, fresh_values)


def step_kernel(
    attn, x, dy, a_ref, b_ref, am_ref, av_ref, bm_ref, bv_ref, w_hbm,
    dec, a_out, b_out, am_out, av_out, bm_out, bv_out,
    w, csend, crecv, ysend, yrecv, zsa, zra, zsb, zrb, yfin,
    one_in, one_z, one_g, one_gr, one_out,
    grad, grad_r, grad_out,
    two_in, two_z, two_g, two_gr, two_out,
    w_sem, c_s, c_r, y_s, y_r, za_s, za_r, zb_s, zb_r, yf_s, yf_r, t_s, t_r,
):
    d = lax.axis_index("dp")
    t = lax.axis_index("tensor")
    z, y, c = t // 4, (t // 2) % 2, t % 2

    def at(zz, yy, cc):
        return (d, (zz * 2 + yy) * 2 + cc)

    core_peer = at(z, y, 1 - c)
    y_peer = at(z, 1 - y, c)
    z_peers = [at(lax.rem(z + k, ZN), y, c) for k in range(1, ZN)]
    group = [core_peer, y_peer, at(z, 1 - y, 1 - c)]
    dp_peers = [(lax.rem(d + k, DP), t) for k in range(1, DP)]

    load_w = pltpu.make_async_copy(w_hbm, w, w_sem)
    load_w.start()

    barrier = pltpu.get_barrier_semaphore()
    everyone = z_peers + group + dp_peers
    for peer in everyone:
        pl.semaphore_signal(barrier, inc=1, device_id=peer, device_id_type=MESH)

    def remote(src, dst, send_sem, recv_sem, peer):
        return pltpu.make_async_remote_copy(
            src_ref=src,
            dst_ref=dst,
            send_sem=send_sem,
            recv_sem=recv_sem,
            device_id=peer,
            device_id_type=MESH,
        )

    class TensorSum:
        def __init__(self, src, z_recv, mine, g_recv, out, first):
            self.src, self.z_recv, self.mine = src, z_recv, mine
            self.g_recv, self.out, self.first = g_recv, out, first
            self.here = pl.ds(pl.multiple_of(z * 32, 32), 32)

        def scatter(self, k):
            part = pl.ds(pl.multiple_of(lax.rem(z + k, ZN) * 32, 32), 32)
            i = self.first + k - 1
            return remote(
                self.src.at[part], self.z_recv.at[k - 1], t_s.at[i], t_r.at[i], z_peers[k - 1]
            )

        def exchange(self, m):
            i = self.first + 7 + m
            return remote(self.mine, self.g_recv.at[m], t_s.at[i], t_r.at[i], group[m])

        def gather(self, k):
            i = self.first + 10 + k - 1
            return remote(
                self.out.at[self.here], self.out.at[self.here], t_s.at[i], t_r.at[i], z_peers[k - 1]
            )

        def one(self):
            for k in range(1, ZN):
                self.scatter(k).start()

        def two(self):
            for k in range(1, ZN):
                self.scatter(k).wait_recv()
            total = self.src[self.here, :]
            for k in range(1, ZN):
                total = total + self.z_recv[k - 1]
            self.mine[...] = total
            for m in range(3):
                self.exchange(m).start()

        def three(self):
            for m in range(3):
                self.exchange(m).wait_recv()
            self.out[self.here, :] = (self.mine[...] + self.g_recv[0]) + (
                self.g_recv[1] + self.g_recv[2]
            )
            for k in range(1, ZN):
                self.gather(k).start()

        def four(self):
            for k in range(1, ZN):
                self.gather(k).wait_recv()

        def finish(self):
            for k in range(1, ZN):
                self.scatter(k).wait_send()
                self.gather(k).wait_send()
            for m in range(3):
                self.exchange(m).wait_send()

    sum_one = TensorSum(one_in, one_z, one_g, one_gr, one_out, 0)
    sum_two = TensorSum(two_in, two_z, two_g, two_gr, two_out, 17)

    a_high, a_low = two_terms(a_ref[...])
    b_high, b_low = two_terms(b_ref[...])
    one_in[...] = jnp.concatenate(
        [
            dot(x[...], a_high) + dot(x[...], a_low),
            dot_t(dy[...], b_high) + dot_t(dy[...], b_low),
        ],
        axis=1,
    )
    pl.semaphore_wait(barrier, len(everyone))
    sum_one.one()

    d_here = pl.ds(pl.multiple_of(d * 16, 16), 16)

    def grad_scatter(k):
        part = pl.ds(pl.multiple_of(lax.rem(d + k, DP) * 16, 16), 16)
        i = 34 + k - 1
        return remote(grad.at[part], grad_r.at[k - 1], t_s.at[i], t_r.at[i], dp_peers[k - 1])

    def grad_gather(k):
        i = 41 + k - 1
        return remote(
            grad_out.at[d_here], grad_out.at[d_here], t_s.at[i], t_r.at[i], dp_peers[k - 1]
        )

    def gradients():
        sum_one.four()
        scale = adapter_scale / (ROWS * DP)
        both = one_out[...].T
        x_high, x_low = two_terms(both[:RANK])
        g_high, g_low = two_terms(both[RANK:])
        grad[:RANK, :] = scale * (dot(g_high, x[...]) + dot(g_low, x[...]))
        grad[RANK:, :] = scale * (dot(x_high, dy[...]) + dot(x_low, dy[...]))
        for k in range(1, DP):
            grad_scatter(k).start()

    def gradient_sum():
        for k in range(1, DP):
            grad_scatter(k).wait_recv()
        total = grad[d_here, :]
        for k in range(1, DP):
            total = total + grad_r[k - 1]
        grad_out[d_here, :] = total
        for k in range(1, DP):
            grad_gather(k).start()

    def update():
        for k in range(1, DP):
            grad_gather(k).wait_recv()
        new_a, a_one, a_two = apply_adam_step(
            a_ref[...], am_ref[...], av_ref[...], grad_out[:RANK, :].T
        )
        a_out[...], am_out[...], av_out[...] = new_a, a_one, a_two
        new_b, b_one, b_two = apply_adam_step(
            b_ref[...], bm_ref[...], bv_ref[...], grad_out[RANK:, :]
        )
        b_out[...], bm_out[...], bv_out[...] = new_b, b_one, b_two
        high, low = two_terms(new_a)
        two_in[...] = dot(attn[...], jnp.concatenate([high, low], axis=1))
        sum_two.one()

    up, down = lax.rem(z + 1, ZN), lax.rem(z + ZN - 1, ZN)
    sides = [at(up, y, c), at(down, y, c)]

    def destination(step, side):
        return lax.rem(z + 2 * ZN - 1 - step, ZN) if side == 0 else lax.rem(z + 1 + step, ZN)

    def product(step, side, other_y, other_c):
        yy = (1 - y) if other_y else y
        cc = (1 - c) if other_c else c
        block = (destination(step, side) * 2 + yy) * 2 + cc
        cols = pl.ds(pl.multiple_of(block * FEAT, FEAT), FEAT)
        return dot(attn[pl.ds(side * HALF, HALF), :], w[:, cols])

    def core_copy(step, side):
        return remote(
            csend.at[step, side], crecv.at[step, side],
            c_s.at[step, side], c_r.at[step, side], core_peer,
        )

    def y_copy(step, side):
        return remote(
            ysend.at[step, side], yrecv.at[step, side],
            y_s.at[step, side], y_r.at[step, side], y_peer,
        )

    def za_copy(step, side):
        return remote(
            zsa.at[step, side], zra.at[step, side],
            za_s.at[step, side], za_r.at[step, side], sides[side],
        )

    def zb_copy(step, side):
        return remote(
            zsb.at[step, side], zrb.at[step, side],
            zb_s.at[step, side], zb_r.at[step, side], sides[side],
        )

    def yfin_copy(side):
        return remote(
            zsa.at[ZN - 1, side, 1], yfin.at[side], yf_s.at[side], yf_r.at[side], y_peer
        )

    def core_stage(step):
        for side in range(2):
            for k in range(2):
                csend[step, side, k] = product(step, side, k == 1, True)
            core_copy(step, side).start()

    def y_stage(step):
        for side in range(2):
            own = product(step, side, False, False)
            other = product(step, side, True, False)
            core_copy(step, side).wait_recv()
            own = own + crecv[step, side, 0]
            other = other + crecv[step, side, 1]
            ysend[step, side] = other[ROWS_A:]
            y_copy(step, side).start()
            zsa[step, side, 0] = own[:ROWS_A]
            zsa[step, side, 1] = other[:ROWS_A]
            zsb[step, side] = own[ROWS_A:]

    def z_stage(step):
        for side in range(2):
            @pl.when(step > 0)
            def _():
                za_copy(step - 1, side).wait_recv()
                zsa[step, side] += zra[step - 1, side]

            @pl.when(step < ZN - 1)
            def _():
                za_copy(step, side).start()

        for side in range(2):
            y_copy(step, side).wait_recv()

            @pl.when(step > 0)
            def _():
                zb_copy(step - 1, side).wait_recv()
                zsb[step, side] += zrb[step - 1, side] + yrecv[step, side]

            @pl.when(step == 0)
            def _():
                zsb[step, side] += yrecv[step, side]

            @pl.when(step < ZN - 1)
            def _():
                zb_copy(step, side).start()

    load_w.wait()
    core_stage(0)
    core_stage(1)
    y_stage(0)
    sum_one.two()

    at_step = {
        0: sum_one.three,
        1: gradients,
        2: gradient_sum,
        3: update,
        4: sum_two.two,
        5: sum_two.three,
    }

    def ring(step, carry):
        z_stage(step)

        @pl.when(step < ZN - 1)
        def _():
            y_stage(step + 1)

        @pl.when(step < ZN - 2)
        def _():
            core_stage(step + 2)

        for when, work in at_step.items():
            pl.when(step == when)(work)
        return carry

    lax.fori_loop(0, ZN, ring, 0)
    for side in range(2):
        yfin_copy(side).start()

    sum_two.four()
    u_high, u_low = two_terms(two_out[...])
    b_high, b_low = two_terms(b_out[...])
    left = jnp.concatenate([u_high, u_low, u_high], axis=1)
    right = jnp.concatenate([b_high, b_high, b_high, b_high, b_low, b_low], axis=0)
    delta = adapter_scale * dot(left, right)

    for side in range(2):
        rows_b = pl.ds(side * HALF + ROWS_A, ROWS_B)
        dec[rows_b, :] = (
            zsb[ZN - 1, side] + delta[side * HALF + ROWS_A : (side + 1) * HALF]
        ).astype(BF16)
    for side in range(2):
        yfin_copy(side).wait_recv()
        rows_a = pl.ds(side * HALF, ROWS_A)
        dec[rows_a, :] = (
            (zsa[ZN - 1, side, 0] + yfin[side]) + delta[side * HALF : side * HALF + ROWS_A]
        ).astype(BF16)

    sum_one.finish()
    sum_two.finish()
    for k in range(1, DP):
        grad_scatter(k).wait_send()
        grad_gather(k).wait_send()
    for side in range(2):
        yfin_copy(side).wait_send()

    def drain(step, carry):
        for side in range(2):
            core_copy(step, side).wait_send()
            y_copy(step, side).wait_send()

            @pl.when(step < ZN - 1)
            def _():
                za_copy(step, side).wait_send()
                zb_copy(step, side).wait_send()

        return carry

    lax.fori_loop(0, ZN, drain, 0)


def step(attn, x, dy, a, b, am, av, bm, bv, weight):
    vmem = pl.BlockSpec(memory_space=pltpu.VMEM)
    down = jax.ShapeDtypeStruct((FEAT, RANK), F32)
    up = jax.ShapeDtypeStruct((RANK, FEAT), F32)
    dma = pltpu.SemaphoreType.DMA
    small = [
        pltpu.VMEM((256, 128), F32),
        pltpu.VMEM((7, 32, 128), F32),
        pltpu.VMEM((32, 128), F32),
        pltpu.VMEM((3, 32, 128), F32),
        pltpu.VMEM((256, 128), F32),
    ]
    return pl.pallas_call(
        step_kernel,
        out_shape=(
            jax.ShapeDtypeStruct((ROWS, FEAT), BF16), down, up, down, down, up, up
        ),
        in_specs=[vmem] * 9 + [pl.BlockSpec(memory_space=pl.ANY)],
        out_specs=(vmem,) * 7,
        scratch_shapes=[
            pltpu.VMEM((FEAT, 8192), BF16),
            pltpu.VMEM((ZN, 2, 2, HALF, FEAT), F32),
            pltpu.VMEM((ZN, 2, 2, HALF, FEAT), F32),
            pltpu.VMEM((ZN, 2, ROWS_B, FEAT), F32),
            pltpu.VMEM((ZN, 2, ROWS_B, FEAT), F32),
            pltpu.VMEM((ZN, 2, 2, ROWS_A, FEAT), F32),
            pltpu.VMEM((ZN - 1, 2, 2, ROWS_A, FEAT), F32),
            pltpu.VMEM((ZN, 2, ROWS_B, FEAT), F32),
            pltpu.VMEM((ZN - 1, 2, ROWS_B, FEAT), F32),
            pltpu.VMEM((2, ROWS_A, FEAT), F32),
            *small,
            pltpu.VMEM((128, FEAT), F32),
            pltpu.VMEM((7, 16, FEAT), F32),
            pltpu.VMEM((128, FEAT), F32),
            *small,
            dma,
            dma((ZN, 2)), dma((ZN, 2)), dma((ZN, 2)), dma((ZN, 2)),
            dma((ZN - 1, 2)), dma((ZN - 1, 2)), dma((ZN - 1, 2)), dma((ZN - 1, 2)),
            dma((2,)), dma((2,)),
            dma((48,)), dma((48,)),
        ],
        compiler_params=pltpu.CompilerParams(
            collective_id=0, has_side_effects=True, vmem_limit_bytes=40 * 1024 * 1024
        ),
    )(attn, x, dy, a, b, am, av, bm, bv, weight)


def per_device(
    projection_input,
    output_gradient,
    adapter_down,
    adapter_up,
    down_first_moment,
    down_second_moment,
    up_first_moment,
    up_second_moment,
    projection_weight,
    queries,
    stored_keys,
    stored_values,
    fresh_keys,
    fresh_values,
    lengths,
):
    attn = attention(
        lengths,
        queries.reshape(ROWS, FEAT),
        stored_keys,
        stored_values,
        fresh_keys.reshape(ROWS, 128),
        fresh_values.reshape(ROWS, 128),
    )
    decoded, *rest = step(
        attn,
        projection_input,
        output_gradient,
        adapter_down,
        adapter_up,
        down_first_moment,
        down_second_moment,
        up_first_moment,
        up_second_moment,
        projection_weight,
    )
    decoded = decoded.reshape(64, 4, FEAT).transpose(1, 0, 2)
    new_a, new_b, a_one, a_two, b_one, b_two = rest
    return (decoded, new_a, new_b, a_one, a_two, b_one, b_two)


def solution(mesh):
    return jax.shard_map(
        per_device,
        mesh=mesh,
        in_specs=(
            P("dp", "tensor"),
            P("dp", "tensor"),
            P("tensor", None),
            P(None, "tensor"),
            P("tensor", None),
            P("tensor", None),
            P(None, "tensor"),
            P(None, "tensor"),
            P("tensor", None),
            P(None, "dp", "tensor"),
            P("dp", None, "tensor"),
            P("dp", None, "tensor"),
            P(None, "dp", "tensor"),
            P(None, "dp", "tensor"),
            P("dp"),
        ),
        out_specs=(
            P(None, "dp", "tensor"),
            P("tensor", None),
            P(None, "tensor"),
            P("tensor", None),
            P("tensor", None),
            P(None, "tensor"),
            P(None, "tensor"),
        ),
        check_vma=False,
    )
```

```python
import functools
import math

import jax
import jax.numpy as jnp
from jax import lax
from jax.experimental import pallas as pl
from jax.experimental.pallas import tpu as pltpu
from jax.sharding import PartitionSpec as P

beta_one = 0.9
beta_two = 0.999
learn_rate = 0.005
adam_count = 10.0
adam_eps = 1e-08
adapter_scale = 2.0

F32 = jnp.float32
BF16 = jnp.bfloat16
MESH = pl.DeviceIdType.MESH

ROWS = 256
FEAT = 256
RANK = 64
ZN = 8
DP = 8
HALF = ROWS // 2
ROWS_A = 64
ROWS_B = HALF - ROWS_A


def apply_adam_step(current, moment_one, moment_two, gradient):
    moment_one = beta_one * moment_one + (1.0 - beta_one) * gradient
    moment_two = beta_two * moment_two + (1.0 - beta_two) * gradient * gradient
    fix_one = 1.0 - beta_one**adam_count
    fix_two = 1.0 - beta_two**adam_count
    updated = current - learn_rate * (moment_one / fix_one) / (
        jnp.sqrt(moment_two / fix_two) + adam_eps
    )
    return (updated, moment_one, moment_two)


def dot(a, b):
    return jnp.dot(a, b, preferred_element_type=F32)


def dot_t(a, b):
    return lax.dot_general(a, b, (((1,), (1,)), ((), ())), preferred_element_type=F32)


def two_terms(a):
    high = a.astype(BF16)
    low = (a - high.astype(F32)).astype(BF16)
    return high, low


class Attention:
    def __init__(self, lengths, q, k, v, fk, fv, out, qs, sc, sn, wc, mixed):
        self.lengths, self.q, self.k, self.v, self.fk, self.fv = lengths, q, k, v, fk, fv
        self.out, self.qs, self.sc, self.sn, self.wc, self.mixed = out, qs, sc, sn, wc, mixed
        self.pairs = k.shape[0] // 2
        i0 = lax.broadcasted_iota(jnp.int32, (ROWS, ROWS), 0)
        i1 = lax.broadcasted_iota(jnp.int32, (ROWS, ROWS), 1)
        self.perm = jnp.where(i1 == (i0 % 4) * 64 + i0 // 4, 1.0, 0.0).astype(BF16)

    def scores(self):
        pairs, qs, sc, sn = self.pairs, self.qs, self.sc, self.sn
        inv_root = 1.0 / math.sqrt(128)
        qp = dot(self.perm, self.q[...])
        qp = jnp.concatenate(
            [qp[:, :128].reshape(pairs, 8, 128), qp[:, 128:].reshape(pairs, 8, 128)], axis=1
        )
        qs[...] = qp.reshape(pairs * 16, 128).astype(BF16)
        fk = dot(self.perm, self.fk[...]).astype(BF16)

        row = lax.broadcasted_iota(jnp.int32, (16, 256), 0)
        col = lax.broadcasted_iota(jnp.int32, (16, 256), 1)
        second = (row // 4) % 2 == 1
        start = jnp.where(second, 128, 0)

        def one_pair(p, carry):
            keys = self.k[pl.ds(2 * p, 2)].reshape(256, 128)
            at = pl.ds(pl.multiple_of(p * 16, 16), 16)
            s = dot_t(qs[at, :], keys) * inv_root
            stop = jnp.where(second, 128 + self.lengths[2 * p + 1], self.lengths[2 * p])
            sc[at, :] = jnp.where((col >= start) & (col < stop), s, -jnp.inf)
            return carry

        lax.fori_loop(0, pairs, one_pair, 0, unroll=8)

        nrow = lax.broadcasted_iota(jnp.int32, (256, 128), 0)
        ncol = lax.broadcasted_iota(jnp.int32, (256, 128), 1)
        request = (nrow // 16) * 2 + (nrow // 4) % 2
        new_live = (ncol // 4 == request) & (ncol % 4 <= nrow % 4)
        for half in range(2):
            part = pl.ds(half * 256, 256)
            s = dot_t(qs[part, :], fk[half * 128 : half * 128 + 128]) * inv_root
            sn[part, :] = jnp.where(new_live, s, -jnp.inf)

    def mix(self):
        pairs, sc, sn, wc, mixed = self.pairs, self.sc, self.sn, self.wc, self.mixed
        fv = dot(self.perm, self.fv[...]).astype(BF16)
        for block in range(8):
            part = pl.ds(block * 64, 64)
            s, n = sc[part, :], sn[part, :]
            largest = jnp.maximum(
                jnp.max(s, axis=1, keepdims=True), jnp.max(n, axis=1, keepdims=True)
            )
            e, m = jnp.exp(s - largest), jnp.exp(n - largest)
            total = jnp.sum(e, axis=1, keepdims=True) + jnp.sum(m, axis=1, keepdims=True)
            scale = 1.0 / total
            wc[part, :] = (e * scale).astype(BF16)
            where_new = (block // 4) * 128
            mixed[part, :] = dot((m * scale).astype(BF16), fv[where_new : where_new + 128])

        def one_pair(p, carry):
            values = self.v[pl.ds(2 * p, 2)].reshape(256, 128)
            at = pl.ds(pl.multiple_of(p * 16, 16), 16)
            mixed[at, :] += dot(wc[at, :], values)
            return carry

        lax.fori_loop(0, pairs, one_pair, 0, unroll=8)
        o = mixed[...].reshape(pairs, 16, 128)
        self.out[:, :128] = o[:, :8].reshape(ROWS, 128).astype(BF16)
        self.out[:, 128:] = o[:, 8:].reshape(ROWS, 128).astype(BF16)


def step_kernel(
    x_h, dy_h, a_h, b_h, len_h, q_h, fk_h, k_h, fv_h, v_h, w_h, am_h, av_h, bm_h, bv_h,
    dec, a_out, b_out, am_out, av_out, bm_out, bv_out,
    x, dy, a_ref, b_ref, lengths, q, fk, keys, fv, values, w, am_ref, av_ref, bm_ref, bv_ref,
    attn, summed, qs, sc, sn, wc, mixed,
    csend, crecv, ysend, yrecv, zsa, zra, zsb, zrb, yfin,
    one_in, one_z, one_g, one_gr, one_out,
    grad, grad_r, grad_out,
    two_in, two_z, two_g, two_gr, two_out,
    in_sem, c_s, c_r, y_s, y_r, za_s, za_r, zb_s, zb_r, yf_s, yf_r, t_s, t_r,
):
    d = lax.axis_index("dp")
    t = lax.axis_index("tensor")
    z, y, c = t // 4, (t // 2) % 2, t % 2

    def at(zz, yy, cc):
        return (d, (zz * 2 + yy) * 2 + cc)

    core_peer = at(z, y, 1 - c)
    y_peer = at(z, 1 - y, c)
    z_peers = [at(lax.rem(z + k, ZN), y, c) for k in range(1, ZN)]
    group = [core_peer, y_peer, at(z, 1 - y, 1 - c)]
    dp_peers = [(lax.rem(d + k, DP), t) for k in range(1, DP)]

    here = (x, dy, a_ref, b_ref, lengths, q, fk, keys, fv, values, w, am_ref, av_ref, bm_ref, bv_ref)
    there = (x_h, dy_h, a_h, b_h, len_h, q_h, fk_h, k_h, fv_h, v_h, w_h, am_h, av_h, bm_h, bv_h)
    loads = [
        pltpu.make_async_copy(src, dst, in_sem.at[i])
        for i, (src, dst) in enumerate(zip(there, here))
    ]
    for load in loads:
        load.start()

    barrier = pltpu.get_barrier_semaphore()
    everyone = z_peers + group + dp_peers
    for peer in everyone:
        pl.semaphore_signal(barrier, inc=1, device_id=peer, device_id_type=MESH)

    def remote(src, dst, send_sem, recv_sem, peer):
        return pltpu.make_async_remote_copy(
            src_ref=src,
            dst_ref=dst,
            send_sem=send_sem,
            recv_sem=recv_sem,
            device_id=peer,
            device_id_type=MESH,
        )

    class TensorSum:
        def __init__(self, src, z_recv, mine, g_recv, out, first):
            self.src, self.z_recv, self.mine = src, z_recv, mine
            self.g_recv, self.out, self.first = g_recv, out, first
            self.here = pl.ds(pl.multiple_of(z * 32, 32), 32)

        def scatter(self, k):
            part = pl.ds(pl.multiple_of(lax.rem(z + k, ZN) * 32, 32), 32)
            i = self.first + k - 1
            return remote(
                self.src.at[part], self.z_recv.at[k - 1], t_s.at[i], t_r.at[i], z_peers[k - 1]
            )

        def exchange(self, m):
            i = self.first + 7 + m
            return remote(self.mine, self.g_recv.at[m], t_s.at[i], t_r.at[i], group[m])

        def gather(self, k):
            i = self.first + 10 + k - 1
            return remote(
                self.out.at[self.here], self.out.at[self.here], t_s.at[i], t_r.at[i], z_peers[k - 1]
            )

        def one(self):
            for k in range(1, ZN):
                self.scatter(k).start()

        def two(self):
            for k in range(1, ZN):
                self.scatter(k).wait_recv()
            total = self.src[self.here, :]
            for k in range(1, ZN):
                total = total + self.z_recv[k - 1]
            self.mine[...] = total
            for m in range(3):
                self.exchange(m).start()

        def three(self):
            for m in range(3):
                self.exchange(m).wait_recv()
            self.out[self.here, :] = (self.mine[...] + self.g_recv[0]) + (
                self.g_recv[1] + self.g_recv[2]
            )
            for k in range(1, ZN):
                self.gather(k).start()

        def four(self):
            for k in range(1, ZN):
                self.gather(k).wait_recv()

        def finish(self):
            for k in range(1, ZN):
                self.scatter(k).wait_send()
                self.gather(k).wait_send()
            for m in range(3):
                self.exchange(m).wait_send()

    sum_one = TensorSum(one_in, one_z, one_g, one_gr, one_out, 0)
    sum_two = TensorSum(two_in, two_z, two_g, two_gr, two_out, 17)

    for load in loads[:4]:
        load.wait()
    a_high, a_low = two_terms(a_ref[...])
    b_high, b_low = two_terms(b_ref[...])
    one_in[...] = jnp.concatenate(
        [
            dot_t(x[...], a_high) + dot_t(x[...], a_low),
            dot_t(dy[...], b_high) + dot_t(dy[...], b_low),
        ],
        axis=1,
    )
    pl.semaphore_wait(barrier, len(everyone))
    sum_one.one()

    d_here = pl.ds(pl.multiple_of(d * 16, 16), 16)

    def grad_scatter(k):
        part = pl.ds(pl.multiple_of(lax.rem(d + k, DP) * 16, 16), 16)
        i = 34 + k - 1
        return remote(grad.at[part], grad_r.at[k - 1], t_s.at[i], t_r.at[i], dp_peers[k - 1])

    def grad_gather(k):
        i = 41 + k - 1
        return remote(
            grad_out.at[d_here], grad_out.at[d_here], t_s.at[i], t_r.at[i], dp_peers[k - 1]
        )

    def gradients():
        sum_one.four()
        scale = adapter_scale / (ROWS * DP)
        both = one_out[...].T
        x_high, x_low = two_terms(both[:RANK])
        g_high, g_low = two_terms(both[RANK:])
        grad[:RANK, :] = scale * (dot(g_high, x[...]) + dot(g_low, x[...]))
        grad[RANK:, :] = scale * (dot(x_high, dy[...]) + dot(x_low, dy[...]))
        for k in range(1, DP):
            grad_scatter(k).start()

    def gradient_sum():
        for k in range(1, DP):
            grad_scatter(k).wait_recv()
        total = grad[d_here, :]
        for k in range(1, DP):
            total = total + grad_r[k - 1]
        grad_out[d_here, :] = total
        for k in range(1, DP):
            grad_gather(k).start()

    def update():
        for k in range(1, DP):
            grad_gather(k).wait_recv()
        new_a, a_one, a_two = apply_adam_step(
            a_ref[...], am_ref[...], av_ref[...], grad_out[:RANK, :]
        )
        a_out[...], am_out[...], av_out[...] = new_a, a_one, a_two
        new_b, b_one, b_two = apply_adam_step(
            b_ref[...], bm_ref[...], bv_ref[...], grad_out[RANK:, :]
        )
        b_out[...], bm_out[...], bv_out[...] = new_b, b_one, b_two
        high, low = two_terms(new_a)
        two_in[...] = dot_t(attn[...], jnp.concatenate([high, low], axis=0))
        sum_two.one()

    up, down = lax.rem(z + 1, ZN), lax.rem(z + ZN - 1, ZN)
    sides = [at(up, y, c), at(down, y, c)]

    def destination(step, side):
        return lax.rem(z + 2 * ZN - 1 - step, ZN) if side == 0 else lax.rem(z + 1 + step, ZN)

    def product(step, side, other_y, other_c):
        yy = (1 - y) if other_y else y
        cc = (1 - c) if other_c else c
        block = (destination(step, side) * 2 + yy) * 2 + cc
        cols = pl.ds(pl.multiple_of(block * FEAT, FEAT), FEAT)
        return dot(attn[pl.ds(side * HALF, HALF), :], w[:, cols])

    def core_copy(step, side):
        return remote(
            csend.at[step, side], crecv.at[step, side],
            c_s.at[step, side], c_r.at[step, side], core_peer,
        )

    def y_copy(step, side):
        return remote(
            ysend.at[step, side], yrecv.at[step, side],
            y_s.at[step, side], y_r.at[step, side], y_peer,
        )

    def za_copy(step, side):
        return remote(
            zsa.at[step, side], zra.at[step, side],
            za_s.at[step, side], za_r.at[step, side], sides[side],
        )

    def zb_copy(step, side):
        return remote(
            zsb.at[step, side], zrb.at[step, side],
            zb_s.at[step, side], zb_r.at[step, side], sides[side],
        )

    def yfin_copy(side):
        return remote(
            zsa.at[ZN - 1, side, 1], yfin.at[side], yf_s.at[side], yf_r.at[side], y_peer
        )

    def core_stage(step):
        for side in range(2):
            for k in range(2):
                csend[step, side, k] = product(step, side, k == 1, True)
            core_copy(step, side).start()

    def y_stage(step):
        for side in range(2):
            own = product(step, side, False, False)
            other = product(step, side, True, False)
            core_copy(step, side).wait_recv()
            own = own + crecv[step, side, 0]
            other = other + crecv[step, side, 1]
            ysend[step, side] = other[ROWS_A:]
            y_copy(step, side).start()
            zsa[step, side, 0] = own[:ROWS_A]
            zsa[step, side, 1] = other[:ROWS_A]
            zsb[step, side] = own[ROWS_A:]

    def z_stage(step):
        for side in range(2):
            @pl.when(step > 0)
            def _():
                za_copy(step - 1, side).wait_recv()
                zsa[step, side] += zra[step - 1, side]

            @pl.when(step < ZN - 1)
            def _():
                za_copy(step, side).start()

        for side in range(2):
            y_copy(step, side).wait_recv()

            @pl.when(step > 0)
            def _():
                zb_copy(step - 1, side).wait_recv()
                zsb[step, side] += zrb[step - 1, side] + yrecv[step, side]

            @pl.when(step == 0)
            def _():
                zsb[step, side] += yrecv[step, side]

            @pl.when(step < ZN - 1)
            def _():
                zb_copy(step, side).start()

    attend = Attention(lengths, q, keys, values, fk, fv, attn, qs, sc, sn, wc, mixed)
    for load in loads[4:8]:
        load.wait()
    attend.scores()
    sum_one.two()
    for load in loads[8:10]:
        load.wait()
    attend.mix()
    sum_one.three()
    loads[10].wait()
    core_stage(0)
    core_stage(1)
    y_stage(0)
    for load in loads[11:]:
        load.wait()

    at_step = {
        0: gradients,
        1: gradient_sum,
        2: update,
        3: sum_two.two,
        4: sum_two.three,
    }

    def ring(step, carry):
        z_stage(step)

        @pl.when(step < ZN - 1)
        def _():
            y_stage(step + 1)

        @pl.when(step < ZN - 2)
        def _():
            core_stage(step + 2)

        for when, work in at_step.items():
            pl.when(step == when)(work)
        return carry

    lax.fori_loop(0, ZN, ring, 0)
    for side in range(2):
        yfin_copy(side).start()

    sum_two.four()
    u_high, u_low = two_terms(two_out[...])
    b_high, b_low = two_terms(b_out[...])
    left = jnp.concatenate([u_high, u_low, u_high], axis=1)
    right = jnp.concatenate([b_high, b_high, b_high, b_high, b_low, b_low], axis=0)
    delta = adapter_scale * dot(left, right)

    for side in range(2):
        rows_b = pl.ds(side * HALF + ROWS_A, ROWS_B)
        summed[rows_b, :] = (
            zsb[ZN - 1, side] + delta[side * HALF + ROWS_A : (side + 1) * HALF]
        ).astype(BF16)
    for side in range(2):
        yfin_copy(side).wait_recv()
        rows_a = pl.ds(side * HALF, ROWS_A)
        summed[rows_a, :] = (
            (zsa[ZN - 1, side, 0] + yfin[side]) + delta[side * HALF : side * HALF + ROWS_A]
        ).astype(BF16)

    back = lax.dot_general(
        attend.perm, summed[...], (((0,), (0,)), ((), ())), preferred_element_type=F32
    )
    dec[...] = back.astype(BF16)

    sum_one.finish()
    sum_two.finish()
    for k in range(1, DP):
        grad_scatter(k).wait_send()
        grad_gather(k).wait_send()
    for side in range(2):
        yfin_copy(side).wait_send()

    def drain(step, carry):
        for side in range(2):
            core_copy(step, side).wait_send()
            y_copy(step, side).wait_send()

            @pl.when(step < ZN - 1)
            def _():
                za_copy(step, side).wait_send()
                zb_copy(step, side).wait_send()

        return carry

    lax.fori_loop(0, ZN, drain, 0)


def step(*args):
    vmem = pl.BlockSpec(memory_space=pltpu.VMEM)
    factor = jax.ShapeDtypeStruct((RANK, FEAT), F32)
    dma = pltpu.SemaphoreType.DMA
    places = [pltpu.SMEM if arg.ndim == 1 else pltpu.VMEM for arg in args]
    small = [
        pltpu.VMEM((256, 128), F32),
        pltpu.VMEM((7, 32, 128), F32),
        pltpu.VMEM((32, 128), F32),
        pltpu.VMEM((3, 32, 128), F32),
        pltpu.VMEM((256, 128), F32),
    ]
    return pl.pallas_call(
        step_kernel,
        out_shape=(jax.ShapeDtypeStruct((ROWS, FEAT), BF16),) + (factor,) * 6,
        in_specs=[pl.BlockSpec(memory_space=pltpu.HBM)] * len(args),
        out_specs=(vmem,) * 7,
        scratch_shapes=[
            *[place(arg.shape, arg.dtype) for place, arg in zip(places, args)],
            pltpu.VMEM((ROWS, FEAT), BF16),
            pltpu.VMEM((ROWS, FEAT), BF16),
            pltpu.VMEM((512, 128), BF16),
            pltpu.VMEM((512, 256), F32),
            pltpu.VMEM((512, 128), F32),
            pltpu.VMEM((512, 256), BF16),
            pltpu.VMEM((512, 128), F32),
            pltpu.VMEM((ZN, 2, 2, HALF, FEAT), F32),
            pltpu.VMEM((ZN, 2, 2, HALF, FEAT), F32),
            pltpu.VMEM((ZN, 2, ROWS_B, FEAT), F32),
            pltpu.VMEM((ZN, 2, ROWS_B, FEAT), F32),
            pltpu.VMEM((ZN, 2, 2, ROWS_A, FEAT), F32),
            pltpu.VMEM((ZN - 1, 2, 2, ROWS_A, FEAT), F32),
            pltpu.VMEM((ZN, 2, ROWS_B, FEAT), F32),
            pltpu.VMEM((ZN - 1, 2, ROWS_B, FEAT), F32),
            pltpu.VMEM((2, ROWS_A, FEAT), F32),
            *small,
            pltpu.VMEM((128, FEAT), F32),
            pltpu.VMEM((7, 16, FEAT), F32),
            pltpu.VMEM((128, FEAT), F32),
            *small,
            dma((len(args),)),
            dma((ZN, 2)), dma((ZN, 2)), dma((ZN, 2)), dma((ZN, 2)),
            dma((ZN - 1, 2)), dma((ZN - 1, 2)), dma((ZN - 1, 2)), dma((ZN - 1, 2)),
            dma((2,)), dma((2,)),
            dma((48,)), dma((48,)),
        ],
        compiler_params=pltpu.CompilerParams(
            collective_id=0, has_side_effects=True, vmem_limit_bytes=64 * 1024 * 1024
        ),
    )(*args)


def hand_out_kernel(*refs):
    half = len(refs) // 2
    copies = [
        pltpu.make_async_copy(src, dst, refs[-1].at[i])
        for i, (src, dst) in enumerate(zip(refs[:half], refs[half:-1]))
    ]
    for copy in copies:
        copy.start()
    for copy in copies:
        copy.wait()


def hand_out(*args):
    return pl.pallas_call(
        hand_out_kernel,
        out_shape=tuple(jax.ShapeDtypeStruct(arg.shape, arg.dtype) for arg in args),
        in_specs=[pl.BlockSpec(memory_space=pl.ANY)] * len(args),
        out_specs=(pl.BlockSpec(memory_space=pltpu.HBM),) * len(args),
        scratch_shapes=[pltpu.SemaphoreType.DMA((len(args),))],
        compiler_params=pltpu.CompilerParams(vmem_limit_bytes=64 * 1024 * 1024),
    )(*args)


def per_device(
    projection_input,
    output_gradient,
    adapter_down,
    adapter_up,
    down_first_moment,
    down_second_moment,
    up_first_moment,
    up_second_moment,
    projection_weight,
    queries,
    stored_keys,
    stored_values,
    fresh_keys,
    fresh_values,
    lengths,
):
    results = step(
        projection_input,
        output_gradient,
        adapter_down.T,
        adapter_up,
        lengths,
        queries.reshape(ROWS, FEAT),
        fresh_keys.reshape(ROWS, 128),
        stored_keys,
        fresh_values.reshape(ROWS, 128),
        stored_values,
        projection_weight,
        down_first_moment.T,
        down_second_moment.T,
        up_first_moment,
        up_second_moment,
    )
    decoded, new_a, new_b, a_one, a_two, b_one, b_two = hand_out(*results)
    return (
        decoded.reshape(queries.shape), new_a.T, new_b, a_one.T, a_two.T, b_one, b_two
    )


def solution(mesh):
    return jax.shard_map(
        per_device,
        mesh=mesh,
        in_specs=(
            P("dp", "tensor"),
            P("dp", "tensor"),
            P("tensor", None),
            P(None, "tensor"),
            P("tensor", None),
            P("tensor", None),
            P(None, "tensor"),
            P(None, "tensor"),
            P("tensor", None),
            P(None, "dp", "tensor"),
            P("dp", None, "tensor"),
            P("dp", None, "tensor"),
            P(None, "dp", "tensor"),
            P(None, "dp", "tensor"),
            P("dp"),
        ),
        out_specs=(
            P(None, "dp", "tensor"),
            P("tensor", None),
            P(None, "tensor"),
            P("tensor", None),
            P("tensor", None),
            P(None, "tensor"),
            P(None, "tensor"),
        ),
        check_vma=False,
    )
```

```python
import functools
import math

import jax
import jax.numpy as jnp
from jax import lax
from jax.experimental import pallas as pl
from jax.experimental.pallas import tpu as pltpu
from jax.sharding import PartitionSpec as P

beta_one = 0.9
beta_two = 0.999
learn_rate = 0.005
adam_count = 10.0
adam_eps = 1e-08
adapter_scale = 2.0

F32 = jnp.float32
BF16 = jnp.bfloat16
MESH = pl.DeviceIdType.MESH

ROWS = 256
FEAT = 256
RANK = 64
ZN = 8
CHIPS = 16
DP = 8
HALF = ROWS // 2
FIRST = 64
STREAMS = (pl.ds(0, FIRST), pl.ds(FIRST, FIRST), pl.ds(2 * FIRST, HALF - FIRST))


def apply_adam_step(current, moment_one, moment_two, gradient):
    moment_one = beta_one * moment_one + (1.0 - beta_one) * gradient
    moment_two = beta_two * moment_two + (1.0 - beta_two) * gradient * gradient
    fix_one = 1.0 - beta_one**adam_count
    fix_two = 1.0 - beta_two**adam_count
    updated = current - learn_rate * (moment_one / fix_one) / (
        jnp.sqrt(moment_two / fix_two) + adam_eps
    )
    return (updated, moment_one, moment_two)


def dot(a, b):
    return jnp.dot(a, b, preferred_element_type=F32)


def dot_t(a, b):
    return lax.dot_general(a, b, (((1,), (1,)), ((), ())), preferred_element_type=F32)


def two_terms(a):
    high = a.astype(BF16)
    low = (a - high.astype(F32)).astype(BF16)
    return high, low


class Attention:
    def __init__(self, lengths, q, k, v, fk, fv, out, qs, sc, sn, wc, mixed):
        self.lengths, self.q, self.k, self.v, self.fk, self.fv = lengths, q, k, v, fk, fv
        self.out, self.qs, self.sc, self.sn, self.wc, self.mixed = out, qs, sc, sn, wc, mixed
        self.pairs = k.shape[0] // 2
        i0 = lax.broadcasted_iota(jnp.int32, (ROWS, ROWS), 0)
        i1 = lax.broadcasted_iota(jnp.int32, (ROWS, ROWS), 1)
        self.perm = jnp.where(i1 == (i0 % 4) * 64 + i0 // 4, 1.0, 0.0).astype(BF16)

    def scores(self):
        pairs, qs, sc, sn = self.pairs, self.qs, self.sc, self.sn
        inv_root = 1.0 / math.sqrt(128)
        qp = dot(self.perm, self.q[...])
        qp = jnp.concatenate(
            [qp[:, :128].reshape(pairs, 8, 128), qp[:, 128:].reshape(pairs, 8, 128)], axis=1
        )
        qs[...] = qp.reshape(pairs * 16, 128).astype(BF16)
        fk = dot(self.perm, self.fk[...]).astype(BF16)

        row = lax.broadcasted_iota(jnp.int32, (16, 256), 0)
        col = lax.broadcasted_iota(jnp.int32, (16, 256), 1)
        second = (row // 4) % 2 == 1
        start = jnp.where(second, 128, 0)

        def one_pair(p, carry):
            keys = self.k[pl.ds(2 * p, 2)].reshape(256, 128)
            at = pl.ds(pl.multiple_of(p * 16, 16), 16)
            s = dot_t(qs[at, :], keys) * inv_root
            stop = jnp.where(second, 128 + self.lengths[2 * p + 1], self.lengths[2 * p])
            sc[at, :] = jnp.where((col >= start) & (col < stop), s, -jnp.inf)
            return carry

        lax.fori_loop(0, pairs, one_pair, 0, unroll=8)

        nrow = lax.broadcasted_iota(jnp.int32, (256, 128), 0)
        ncol = lax.broadcasted_iota(jnp.int32, (256, 128), 1)
        request = (nrow // 16) * 2 + (nrow // 4) % 2
        new_live = (ncol // 4 == request) & (ncol % 4 <= nrow % 4)
        for half in range(2):
            part = pl.ds(half * 256, 256)
            s = dot_t(qs[part, :], fk[half * 128 : half * 128 + 128]) * inv_root
            sn[part, :] = jnp.where(new_live, s, -jnp.inf)

    def mix(self):
        pairs, sc, sn, wc, mixed = self.pairs, self.sc, self.sn, self.wc, self.mixed
        fv = dot(self.perm, self.fv[...]).astype(BF16)
        for block in range(8):
            part = pl.ds(block * 64, 64)
            s, n = sc[part, :], sn[part, :]
            largest = jnp.maximum(
                jnp.max(s, axis=1, keepdims=True), jnp.max(n, axis=1, keepdims=True)
            )
            e, m = jnp.exp(s - largest), jnp.exp(n - largest)
            total = jnp.sum(e, axis=1, keepdims=True) + jnp.sum(m, axis=1, keepdims=True)
            scale = 1.0 / total
            wc[part, :] = (e * scale).astype(BF16)
            where_new = (block // 4) * 128
            mixed[part, :] = dot((m * scale).astype(BF16), fv[where_new : where_new + 128])

        def one_pair(p, carry):
            values = self.v[pl.ds(2 * p, 2)].reshape(256, 128)
            at = pl.ds(pl.multiple_of(p * 16, 16), 16)
            mixed[at, :] += dot(wc[at, :], values)
            return carry

        lax.fori_loop(0, pairs, one_pair, 0, unroll=8)
        o = mixed[...].reshape(pairs, 16, 128)
        self.out[:, :128] = o[:, :8].reshape(ROWS, 128).astype(BF16)
        self.out[:, 128:] = o[:, 8:].reshape(ROWS, 128).astype(BF16)


def step_kernel(
    x_h, dy_h, a_h, b_h, len_h, q_h, fk_h, k_h, fv_h, v_h, w_h, am_h, av_h, bm_h, bv_h,
    dec, a_out, b_out, am_out, av_out, bm_out, bv_out,
    x, dy, a_ref, b_ref, lengths, q, fk, keys, fv, values, w, am_ref, av_ref, bm_ref, bv_ref,
    attn, summed, qs, sc, sn, wc, mixed,
    csend, crecv, ysend, yrecv, zs, zr, yfin_src, yfin,
    one_in, one_core, one_half, one_recv, one_out,
    grad, grad_r, grad_out,
    two_in, two_core, two_half, two_recv, two_out,
    in_sem, c_s, c_r, y_s, y_r, z_s, z_r, yf_s, yf_r, t_s, t_r,
):
    d = lax.axis_index("dp")
    t = lax.axis_index("tensor")
    z, y, c = t // 4, (t // 2) % 2, t % 2

    def at(zz, yy, cc):
        return (d, (zz * 2 + yy) * 2 + cc)

    core_peer = at(z, y, 1 - c)
    y_peer = at(z, 1 - y, c)
    chip = z * 2 + y
    chip_peers = [(d, lax.rem(chip + k, CHIPS) * 2 + c) for k in range(1, CHIPS)]
    dp_peers = [(lax.rem(d + k, DP), t) for k in range(1, DP)]

    here = (x, dy, a_ref, b_ref, lengths, q, fk, keys, fv, values, w, am_ref, av_ref, bm_ref, bv_ref)
    there = (x_h, dy_h, a_h, b_h, len_h, q_h, fk_h, k_h, fv_h, v_h, w_h, am_h, av_h, bm_h, bv_h)
    loads = [
        pltpu.make_async_copy(src, dst, in_sem.at[i])
        for i, (src, dst) in enumerate(zip(there, here))
    ]
    for load in loads:
        load.start()

    barrier = pltpu.get_barrier_semaphore()
    everyone = chip_peers + [core_peer] + dp_peers
    for peer in everyone:
        pl.semaphore_signal(barrier, inc=1, device_id=peer, device_id_type=MESH)

    def remote(src, dst, send_sem, recv_sem, peer):
        return pltpu.make_async_remote_copy(
            src_ref=src,
            dst_ref=dst,
            send_sem=send_sem,
            recv_sem=recv_sem,
            device_id=peer,
            device_id_type=MESH,
        )

    class TensorSum:
        def __init__(self, src, core_recv, half, recv, out, first):
            self.src, self.core_recv, self.half = src, core_recv, half
            self.recv, self.out, self.first = recv, out, first
            self.mine = pl.ds(pl.multiple_of(c * 128, 128), 128)
            self.theirs = pl.ds(pl.multiple_of((1 - c) * 128, 128), 128)
            self.part = pl.ds(pl.multiple_of(chip * 8, 8), 8)
            self.here = pl.ds(pl.multiple_of(c * 128 + chip * 8, 8), 8)

        def core_scatter(self):
            i = self.first
            return remote(self.src.at[self.theirs], self.core_recv, t_s.at[i], t_r.at[i], core_peer)

        def scatter(self, k):
            part = pl.ds(pl.multiple_of(lax.rem(chip + k, CHIPS) * 8, 8), 8)
            i = self.first + k
            return remote(
                self.half.at[part], self.recv.at[k - 1], t_s.at[i], t_r.at[i], chip_peers[k - 1]
            )

        def gather(self, k):
            i = self.first + 15 + k
            return remote(
                self.out.at[self.here], self.out.at[self.here],
                t_s.at[i], t_r.at[i], chip_peers[k - 1],
            )

        def core_gather(self):
            i = self.first + 31
            return remote(
                self.out.at[self.mine], self.out.at[self.mine], t_s.at[i], t_r.at[i], core_peer
            )

        def one(self):
            self.core_scatter().start()

        def two(self):
            self.core_scatter().wait_recv()
            self.half[...] = self.src[self.mine, :] + self.core_recv[...]
            for k in range(1, CHIPS):
                self.scatter(k).start()

        def three(self):
            for k in range(1, CHIPS):
                self.scatter(k).wait_recv()
            total = self.half[self.part, :]
            for k in range(1, CHIPS):
                total = total + self.recv[k - 1]
            self.out[self.here, :] = total
            for k in range(1, CHIPS):
                self.gather(k).start()

        def four(self):
            for k in range(1, CHIPS):
                self.gather(k).wait_recv()
            self.core_gather().start()

        def five(self):
            self.core_gather().wait_recv()

        def finish(self):
            self.core_scatter().wait_send()
            self.core_gather().wait_send()
            for k in range(1, CHIPS):
                self.scatter(k).wait_send()
                self.gather(k).wait_send()

    sum_one = TensorSum(one_in, one_core, one_half, one_recv, one_out, 0)
    sum_two = TensorSum(two_in, two_core, two_half, two_recv, two_out, 32)

    for load in loads[:4]:
        load.wait()
    a_high, a_low = two_terms(a_ref[...])
    b_high, b_low = two_terms(b_ref[...])
    one_in[...] = jnp.concatenate(
        [
            dot_t(x[...], a_high) + dot_t(x[...], a_low),
            dot_t(dy[...], b_high) + dot_t(dy[...], b_low),
        ],
        axis=1,
    )
    pl.semaphore_wait(barrier, len(everyone))
    sum_one.one()

    d_here = pl.ds(pl.multiple_of(d * 16, 16), 16)

    def grad_scatter(k):
        part = pl.ds(pl.multiple_of(lax.rem(d + k, DP) * 16, 16), 16)
        i = 64 + k - 1
        return remote(grad.at[part], grad_r.at[k - 1], t_s.at[i], t_r.at[i], dp_peers[k - 1])

    def grad_gather(k):
        i = 71 + k - 1
        return remote(
            grad_out.at[d_here], grad_out.at[d_here], t_s.at[i], t_r.at[i], dp_peers[k - 1]
        )

    def gradients():
        sum_one.five()
        scale = adapter_scale / (ROWS * DP)
        both = one_out[...].T
        x_high, x_low = two_terms(both[:RANK])
        g_high, g_low = two_terms(both[RANK:])
        grad[:RANK, :] = scale * (dot(g_high, x[...]) + dot(g_low, x[...]))
        grad[RANK:, :] = scale * (dot(x_high, dy[...]) + dot(x_low, dy[...]))
        for k in range(1, DP):
            grad_scatter(k).start()

    def gradient_sum():
        for k in range(1, DP):
            grad_scatter(k).wait_recv()
        total = grad[d_here, :]
        for k in range(1, DP):
            total = total + grad_r[k - 1]
        grad_out[d_here, :] = total
        for k in range(1, DP):
            grad_gather(k).start()

    def update():
        for k in range(1, DP):
            grad_gather(k).wait_recv()
        new_a, a_one, a_two = apply_adam_step(
            a_ref[...], am_ref[...], av_ref[...], grad_out[:RANK, :]
        )
        a_out[...], am_out[...], av_out[...] = new_a, a_one, a_two
        high, low = two_terms(new_a)
        two_in[...] = dot_t(attn[...], jnp.concatenate([high, low], axis=0))
        sum_two.one()
        new_b, b_one, b_two = apply_adam_step(
            b_ref[...], bm_ref[...], bv_ref[...], grad_out[RANK:, :]
        )
        b_out[...], bm_out[...], bv_out[...] = new_b, b_one, b_two

    ways = [at(lax.rem(z + 1, ZN), y, c), at(lax.rem(z + ZN - 1, ZN), y, c)]

    def product(u, other_y, other_c):
        yy = (1 - y) if other_y else y
        cc = (1 - c) if other_c else c
        to = lax.rem(z + ZN + 4 + (1 - 2 * lax.rem(u, 2)) * ((u + 1) // 2), ZN)
        block = (to * 2 + yy) * 2 + cc
        cols = pl.ds(pl.multiple_of(block * FEAT, FEAT), FEAT)
        return dot(attn[...], w[:, cols])

    def core_copy(u):
        return remote(csend.at[u], crecv.at[u], c_s.at[u], c_r.at[u], core_peer)

    def y_copy(u):
        return remote(ysend.at[u], yrecv.at[u], y_s.at[u], y_r.at[u], y_peer)

    def core_stage(u):
        for k in range(2):
            csend[u, k] = product(u, k == 1, True)
        core_copy(u).start()

    def y_stage(u):
        own = product(u, False, False)
        other = product(u, True, False)
        core_copy(u).wait_recv()
        own = own + crecv[u, 0]
        other = other + crecv[u, 1]
        for half in range(2):
            low, mid, high = half * HALF, half * HALF + FIRST, (half + 1) * HALF
            ysend[u, half] = other[mid:high]
            zs[u, half, STREAMS[0], :] = other[low:mid]
            zs[u, half, STREAMS[1], :] = own[low:mid]
            zs[u, half, STREAMS[2], :] = own[mid:high]
        y_copy(u).start()

    def y_add(u):
        y_copy(u).wait_recv()
        for half in range(2):
            zs[u, half, STREAMS[2], :] += yrecv[u, half]

    def unit(step, way):
        return 0 if step == 0 else 2 * step - 1 + way

    def z_copy(step, way, half, stream):
        return remote(
            zs.at[unit(step, way), half, STREAMS[stream]],
            zr.at[step, way, half, STREAMS[stream]],
            z_s.at[step, way, half, stream],
            z_r.at[step, way, half, stream],
            ways[way],
        )

    def z_send(step, stream, late):
        for way in range(2):
            half = way if late else 1 - way
            if step > 0 and (late or step > 1):
                z_copy(step - 1, way, half, stream).wait_recv()
                rows = STREAMS[stream]
                zs[unit(step, way), half, rows, :] += zr[step - 1, way, half, rows, :]
            z_copy(step, way, half, stream).start()

    def z_end(stream):
        rows = STREAMS[stream]
        for half in range(2):
            for way in range(2):
                z_copy(3, way, half, stream).wait_recv()
            zs[7, half, rows, :] += zr[3, 0, half, rows, :] + zr[3, 1, half, rows, :]

    def yfin_copy():
        return remote(yfin_src, yfin, yf_s, yf_r, y_peer)

    attend = Attention(lengths, q, keys, values, fk, fv, attn, qs, sc, sn, wc, mixed)
    for load in loads[4:8]:
        load.wait()
    sum_one.two()
    attend.scores()
    for load in loads[8:10]:
        load.wait()
    attend.mix()
    loads[10].wait()

    def next_units(u, carry):
        core_stage(u + 2)
        y_stage(u)
        return carry

    core_stage(0)
    core_stage(1)
    core_stage(2)
    sum_one.three()
    y_stage(0)
    z_send(0, 0, True)
    z_send(0, 1, True)
    lax.fori_loop(1, 3, next_units, 0)
    z_send(1, 0, False)
    z_send(1, 1, False)
    y_add(0)
    z_send(0, 2, True)
    z_send(1, 0, True)
    z_send(1, 1, True)
    sum_one.four()
    gradients()
    lax.fori_loop(3, 5, next_units, 0)
    y_add(1)
    y_add(2)
    z_send(1, 2, False)
    z_send(1, 2, True)
    for load in loads[11:]:
        load.wait()
    z_send(2, 0, False)
    z_send(2, 0, True)
    z_send(2, 1, False)
    z_send(2, 1, True)
    gradient_sum()
    next_units(5, 0)
    lax.fori_loop(6, 8, lambda u, carry: (y_stage(u), carry)[1], 0)
    y_add(3)
    y_add(4)
    z_send(2, 2, False)
    z_send(2, 2, True)
    update()
    sum_two.two()
    z_send(3, 0, False)
    z_send(3, 0, True)
    z_send(3, 1, False)
    z_send(3, 1, True)
    y_add(5)
    y_add(6)
    sum_two.three()
    z_send(3, 2, False)
    z_send(3, 2, True)
    z_end(0)
    for half in range(2):
        yfin_src[half] = zs[7, half, STREAMS[0], :]
    yfin_copy().start()
    z_end(1)
    sum_two.four()
    y_add(7)
    z_end(2)
    sum_two.five()
    u_high, u_low = two_terms(two_out[...])
    b_high, b_low = two_terms(b_out[...])
    left = jnp.concatenate([u_high, u_low, u_high], axis=1)
    right = jnp.concatenate([b_high, b_high, b_high, b_high, b_low, b_low], axis=0)
    delta = adapter_scale * dot(left, right)

    yfin_copy().wait_recv()
    for half in range(2):
        low, mid, high = half * HALF, half * HALF + FIRST, (half + 1) * HALF
        summed[pl.ds(low, FIRST), :] = (
            (zs[7, half, STREAMS[1], :] + yfin[half]) + delta[low:mid]
        ).astype(BF16)
        summed[pl.ds(mid, HALF - FIRST), :] = (
            zs[7, half, STREAMS[2], :] + delta[mid:high]
        ).astype(BF16)
    back = lax.dot_general(
        attend.perm, summed[...], (((0,), (0,)), ((), ())), preferred_element_type=F32
    )
    dec[...] = back.astype(BF16)

    sum_one.finish()
    sum_two.finish()
    for k in range(1, DP):
        grad_scatter(k).wait_send()
        grad_gather(k).wait_send()
    yfin_copy().wait_send()
    for u in range(8):
        core_copy(u).wait_send()
        y_copy(u).wait_send()
    for way in range(2):
        for stream in range(3):
            z_copy(0, way, way, stream).wait_send()
            for after in range(1, 4):
                for half in range(2):
                    z_copy(after, way, half, stream).wait_send()


def step(*args):
    vmem = pl.BlockSpec(memory_space=pltpu.VMEM)
    factor = jax.ShapeDtypeStruct((RANK, FEAT), F32)
    dma = pltpu.SemaphoreType.DMA
    places = [pltpu.SMEM if arg.ndim == 1 else pltpu.VMEM for arg in args]
    small = [
        pltpu.VMEM((256, 128), F32),
        pltpu.VMEM((128, 128), F32),
        pltpu.VMEM((128, 128), F32),
        pltpu.VMEM((CHIPS - 1, 8, 128), F32),
        pltpu.VMEM((256, 128), F32),
    ]
    return pl.pallas_call(
        step_kernel,
        out_shape=(jax.ShapeDtypeStruct((ROWS, FEAT), BF16),) + (factor,) * 6,
        in_specs=[pl.BlockSpec(memory_space=pltpu.HBM)] * len(args),
        out_specs=(vmem,) * 7,
        scratch_shapes=[
            *[place(arg.shape, arg.dtype) for place, arg in zip(places, args)],
            pltpu.VMEM((ROWS, FEAT), BF16),
            pltpu.VMEM((ROWS, FEAT), BF16),
            pltpu.VMEM((512, 128), BF16),
            pltpu.VMEM((512, 256), F32),
            pltpu.VMEM((512, 128), F32),
            pltpu.VMEM((512, 256), BF16),
            pltpu.VMEM((512, 128), F32),
            pltpu.VMEM((8, 2, ROWS, FEAT), F32),
            pltpu.VMEM((8, 2, ROWS, FEAT), F32),
            pltpu.VMEM((8, 2, HALF - FIRST, FEAT), F32),
            pltpu.VMEM((8, 2, HALF - FIRST, FEAT), F32),
            pltpu.VMEM((8, 2, HALF + FIRST, FEAT), F32),
            pltpu.VMEM((4, 2, 2, HALF + FIRST, FEAT), F32),
            pltpu.VMEM((2, FIRST, FEAT), F32),
            pltpu.VMEM((2, FIRST, FEAT), F32),
            *small,
            pltpu.VMEM((128, FEAT), F32),
            pltpu.VMEM((7, 16, FEAT), F32),
            pltpu.VMEM((128, FEAT), F32),
            *small,
            dma((len(args),)),
            dma((8,)), dma((8,)), dma((8,)), dma((8,)),
            dma((4, 2, 2, 3)), dma((4, 2, 2, 3)),
            dma, dma,
            dma((78,)), dma((78,)),
        ],
        compiler_params=pltpu.CompilerParams(
            collective_id=0, has_side_effects=True, vmem_limit_bytes=64 * 1024 * 1024
        ),
    )(*args)


def hand_out_kernel(*refs):
    half = len(refs) // 2
    for src, dst in zip(refs[:half], refs[half:]):
        dst[...] = src[...]


def hand_out(*args):
    vmem = pl.BlockSpec(memory_space=pltpu.VMEM)
    return pl.pallas_call(
        hand_out_kernel,
        out_shape=tuple(jax.ShapeDtypeStruct(arg.shape, arg.dtype) for arg in args),
        in_specs=[vmem] * len(args),
        out_specs=(vmem,) * len(args),
        compiler_params=pltpu.CompilerParams(vmem_limit_bytes=64 * 1024 * 1024),
    )(*args)


def per_device(
    projection_input,
    output_gradient,
    adapter_down,
    adapter_up,
    down_first_moment,
    down_second_moment,
    up_first_moment,
    up_second_moment,
    projection_weight,
    queries,
    stored_keys,
    stored_values,
    fresh_keys,
    fresh_values,
    lengths,
):
    results = step(
        projection_input,
        output_gradient,
        adapter_down.T,
        adapter_up,
        lengths,
        queries.reshape(ROWS, FEAT),
        fresh_keys.reshape(ROWS, 128),
        stored_keys,
        fresh_values.reshape(ROWS, 128),
        stored_values,
        projection_weight,
        down_first_moment.T,
        down_second_moment.T,
        up_first_moment,
        up_second_moment,
    )
    decoded, new_a, new_b, a_one, a_two, b_one, b_two = hand_out(*results)
    return (
        decoded.reshape(queries.shape), new_a.T, new_b, a_one.T, a_two.T, b_one, b_two
    )


def solution(mesh):
    return jax.shard_map(
        per_device,
        mesh=mesh,
        in_specs=(
            P("dp", "tensor"),
            P("dp", "tensor"),
            P("tensor", None),
            P(None, "tensor"),
            P("tensor", None),
            P("tensor", None),
            P(None, "tensor"),
            P(None, "tensor"),
            P("tensor", None),
            P(None, "dp", "tensor"),
            P("dp", None, "tensor"),
            P("dp", None, "tensor"),
            P(None, "dp", "tensor"),
            P(None, "dp", "tensor"),
            P("dp"),
        ),
        out_specs=(
            P(None, "dp", "tensor"),
            P("tensor", None),
            P(None, "tensor"),
            P("tensor", None),
            P("tensor", None),
            P(None, "tensor"),
            P(None, "tensor"),
        ),
        check_vma=False,
    )
```

```python
import functools
import math

import jax
import jax.numpy as jnp
from jax import lax
from jax.experimental import pallas as pl
from jax.experimental.pallas import tpu as pltpu
from jax.sharding import PartitionSpec as P

beta_one = 0.9
beta_two = 0.999
learn_rate = 0.005
adam_count = 10.0
adam_eps = 1e-08
adapter_scale = 2.0

F32 = jnp.float32
BF16 = jnp.bfloat16
MESH = pl.DeviceIdType.MESH

ROWS = 256
FEAT = 256
RANK = 64
ZN = 8
CHIPS = 16
DP = 8
HALF = ROWS // 2
FIRST = 64
STREAMS = (pl.ds(0, FIRST), pl.ds(FIRST, FIRST), pl.ds(2 * FIRST, HALF - FIRST))


def apply_adam_step(current, moment_one, moment_two, gradient):
    moment_one = beta_one * moment_one + (1.0 - beta_one) * gradient
    moment_two = beta_two * moment_two + (1.0 - beta_two) * gradient * gradient
    fix_one = 1.0 - beta_one**adam_count
    fix_two = 1.0 - beta_two**adam_count
    updated = current - learn_rate * (moment_one / fix_one) / (
        jnp.sqrt(moment_two / fix_two) + adam_eps
    )
    return (updated, moment_one, moment_two)


def dot(a, b):
    return jnp.dot(a, b, preferred_element_type=F32)


def dot_t(a, b):
    return lax.dot_general(a, b, (((1,), (1,)), ((), ())), preferred_element_type=F32)


def two_terms(a):
    high = a.astype(BF16)
    low = (a - high.astype(F32)).astype(BF16)
    return high, low


class Attention:
    def __init__(self, lengths, q, k, v, fk, fv, out, qs, sc, sn, mixed):
        self.lengths, self.q, self.k, self.v, self.fk, self.fv = lengths, q, k, v, fk, fv
        self.out, self.qs, self.sc, self.sn, self.mixed = out, qs, sc, sn, mixed
        self.pairs = k.shape[0] // 2
        i0 = lax.broadcasted_iota(jnp.int32, (ROWS, ROWS), 0)
        i1 = lax.broadcasted_iota(jnp.int32, (ROWS, ROWS), 1)
        self.perm = jnp.where(i1 == (i0 % 4) * 64 + i0 // 4, 1.0, 0.0).astype(BF16)
        self.back = jnp.where(i0 == (i1 % 4) * 64 + i1 // 4, 1.0, 0.0).astype(BF16)

    def scores(self):
        pairs, qs, sc, sn = self.pairs, self.qs, self.sc, self.sn
        inv_root = 1.0 / math.sqrt(128)
        qp = dot(self.perm, self.q[...])
        qp = jnp.concatenate(
            [qp[:, :128].reshape(pairs, 8, 128), qp[:, 128:].reshape(pairs, 8, 128)], axis=1
        )
        qs[...] = qp.reshape(pairs * 16, 128).astype(BF16)
        fk = dot(self.perm, self.fk[...]).astype(BF16)

        row = lax.broadcasted_iota(jnp.int32, (16, 256), 0)
        col = lax.broadcasted_iota(jnp.int32, (16, 256), 1)
        second = (row // 4) % 2 == 1
        start = jnp.where(second, 128, 0)

        def one_pair(p, carry):
            keys = self.k[pl.ds(2 * p, 2)].reshape(256, 128)
            at = pl.ds(pl.multiple_of(p * 16, 16), 16)
            s = dot_t(qs[at, :], keys) * inv_root
            stop = jnp.where(second, 128 + self.lengths[2 * p + 1], self.lengths[2 * p])
            sc[at, :] = jnp.where((col >= start) & (col < stop), s, -jnp.inf)
            return carry

        lax.fori_loop(0, pairs, one_pair, 0, unroll=32)

        nrow = lax.broadcasted_iota(jnp.int32, (256, 128), 0)
        ncol = lax.broadcasted_iota(jnp.int32, (256, 128), 1)
        request = (nrow // 16) * 2 + (nrow // 4) % 2
        new_live = (ncol // 4 == request) & (ncol % 4 <= nrow % 4)
        for half in range(2):
            part = pl.ds(half * 256, 256)
            s = dot_t(qs[part, :], fk[half * 128 : half * 128 + 128]) * inv_root
            sn[part, :] = jnp.where(new_live, s, -jnp.inf)

    def mix(self):
        sc, sn, mixed = self.sc, self.sn, self.mixed
        pairs = self.pairs
        fv = dot(self.perm, self.fv[...]).astype(BF16)
        for block in range(8):
            part = pl.ds(block * 64, 64)
            s, n = sc[part, :], sn[part, :]
            largest = jnp.maximum(
                jnp.max(s, axis=1, keepdims=True), jnp.max(n, axis=1, keepdims=True)
            )
            e, m = jnp.exp(s - largest), jnp.exp(n - largest)
            total = jnp.sum(e, axis=1, keepdims=True) + jnp.sum(m, axis=1, keepdims=True)
            scale = 1.0 / total
            weights = (e * scale).astype(BF16)
            where_new = (block // 4) * 128
            new = dot((m * scale).astype(BF16), fv[where_new : where_new + 128])
            for i in range(4):
                p = block * 4 + i
                values = self.v[2 * p : 2 * p + 2].reshape(256, 128)
                mixed[p * 16 : p * 16 + 16, :] = (
                    dot(weights[i * 16 : i * 16 + 16], values) + new[i * 16 : i * 16 + 16]
                )
        o = mixed[...].reshape(pairs, 16, 128)
        o = jnp.concatenate(
            [o[:, :8].reshape(ROWS, 128), o[:, 8:].reshape(ROWS, 128)], axis=1
        ).astype(BF16)
        self.out[...] = dot(self.back, o).astype(BF16)


def step_kernel(
    x_h, dy_h, a_h, b_h, len_h, q_h, fk_h, k_h, fv_h, v_h, w_h, am_h, av_h, bm_h, bv_h,
    dec, a_out, b_out, am_out, av_out, bm_out, bv_out,
    x, dy, a_ref, b_ref, lengths, q, fk, keys, fv, values, w, am_ref, av_ref, bm_ref, bv_ref,
    attn, base, right, qs, sc, sn, mixed,
    csend, crecv, ysend, yrecv, zs, zr, yfin_src, yfin,
    one_in, one_core, one_half, one_recv, one_out,
    grad, grad_r, grad_out,
    two_in, two_core, two_half, two_recv, two_out,
    in_sem, c_s, c_r, y_s, y_r, z_s, z_r, yf_s, yf_r, t_s, t_r,
):
    d = lax.axis_index("dp")
    t = lax.axis_index("tensor")
    z, y, c = t // 4, (t // 2) % 2, t % 2

    def at(zz, yy, cc):
        return (d, (zz * 2 + yy) * 2 + cc)

    core_peer = at(z, y, 1 - c)
    y_peer = at(z, 1 - y, c)
    chip = z * 2 + y
    chip_peers = [(d, lax.rem(chip + k, CHIPS) * 2 + c) for k in range(1, CHIPS)]
    dp_peers = [(lax.rem(d + k, DP), t) for k in range(1, DP)]

    barrier = pltpu.get_barrier_semaphore()
    everyone = chip_peers[7:] + chip_peers[:7][::-1] + dp_peers + [core_peer]
    for peer in everyone:
        pl.semaphore_signal(barrier, inc=1, device_id=peer, device_id_type=MESH)

    here = (x, dy, a_ref, b_ref, lengths, q, fk, keys, fv, values, w, am_ref, av_ref, bm_ref, bv_ref)
    there = (x_h, dy_h, a_h, b_h, len_h, q_h, fk_h, k_h, fv_h, v_h, w_h, am_h, av_h, bm_h, bv_h)
    loads = [
        pltpu.make_async_copy(src, dst, in_sem.at[i])
        for i, (src, dst) in enumerate(zip(there, here))
    ]
    for load in loads[:8]:
        load.start()

    def remote(src, dst, send_sem, recv_sem, peer):
        return pltpu.make_async_remote_copy(
            src_ref=src,
            dst_ref=dst,
            send_sem=send_sem,
            recv_sem=recv_sem,
            device_id=peer,
            device_id_type=MESH,
        )

    class TensorSum:
        def __init__(self, src, core_recv, half, recv, out, first):
            self.src, self.core_recv, self.half = src, core_recv, half
            self.recv, self.out, self.first = recv, out, first
            self.mine = pl.ds(pl.multiple_of(c * 128, 128), 128)
            self.theirs = pl.ds(pl.multiple_of((1 - c) * 128, 128), 128)
            self.part = pl.ds(pl.multiple_of(chip * 8, 8), 8)
            self.here = pl.ds(pl.multiple_of(c * 128 + chip * 8, 8), 8)

        def core_scatter(self):
            i = self.first
            return remote(self.src.at[self.theirs], self.core_recv, t_s.at[i], t_r.at[i], core_peer)

        def scatter(self, k):
            part = pl.ds(pl.multiple_of(lax.rem(chip + k, CHIPS) * 8, 8), 8)
            i = self.first + k
            return remote(
                self.half.at[part], self.recv.at[k - 1], t_s.at[i], t_r.at[i], chip_peers[k - 1]
            )

        def gather(self, k):
            i = self.first + 15 + k
            return remote(
                self.out.at[self.here], self.out.at[self.here],
                t_s.at[i], t_r.at[i], chip_peers[k - 1],
            )

        def core_gather(self):
            i = self.first + 31
            return remote(
                self.out.at[self.mine], self.out.at[self.mine], t_s.at[i], t_r.at[i], core_peer
            )

        def one(self):
            self.core_scatter().start()

        def two(self):
            self.core_scatter().wait_recv()
            self.half[...] = self.src[self.mine, :] + self.core_recv[...]
            for k in range(1, CHIPS):
                self.scatter(k).start()

        def three(self):
            for k in range(1, CHIPS):
                self.scatter(k).wait_recv()
            total = self.half[self.part, :]
            for k in range(1, CHIPS):
                total = total + self.recv[k - 1]
            self.out[self.here, :] = total
            for k in range(1, CHIPS):
                self.gather(k).start()

        def four(self):
            for k in range(1, CHIPS):
                self.gather(k).wait_recv()
            self.core_gather().start()

        def five(self):
            self.core_gather().wait_recv()

        def finish(self):
            self.core_scatter().wait_send()
            self.core_gather().wait_send()
            for k in range(1, CHIPS):
                self.scatter(k).wait_send()
                self.gather(k).wait_send()

    sum_one = TensorSum(one_in, one_core, one_half, one_recv, one_out, 0)
    sum_two = TensorSum(two_in, two_core, two_half, two_recv, two_out, 32)

    for load in loads[:4]:
        load.wait()
    for load in loads[8:11]:
        load.start()
    a_high, a_low = two_terms(a_ref[...])
    b_high, b_low = two_terms(b_ref[...])
    one_in[...] = jnp.concatenate(
        [
            dot_t(x[...], a_high) + dot_t(x[...], a_low),
            dot_t(dy[...], b_high) + dot_t(dy[...], b_low),
        ],
        axis=1,
    )
    pl.semaphore_wait(barrier, len(everyone))
    sum_one.one()

    d_here = pl.ds(pl.multiple_of(d * 16, 16), 16)

    def grad_scatter(k):
        part = pl.ds(pl.multiple_of(lax.rem(d + k, DP) * 16, 16), 16)
        i = 64 + k - 1
        return remote(grad.at[part], grad_r.at[k - 1], t_s.at[i], t_r.at[i], dp_peers[k - 1])

    def grad_gather(k):
        i = 71 + k - 1
        return remote(
            grad_out.at[d_here], grad_out.at[d_here], t_s.at[i], t_r.at[i], dp_peers[k - 1]
        )

    def gradients():
        sum_one.five()
        scale = adapter_scale / (ROWS * DP)
        both = one_out[...].T
        x_high, x_low = two_terms(both[:RANK])
        g_high, g_low = two_terms(both[RANK:])
        grad[:RANK, :] = scale * (dot(g_high, x[...]) + dot(g_low, x[...]))
        grad[RANK:, :] = scale * (dot(x_high, dy[...]) + dot(x_low, dy[...]))
        for k in range(1, DP):
            grad_scatter(k).start()

    def gradient_sum():
        for k in range(1, DP):
            grad_scatter(k).wait_recv()
        total = grad[d_here, :]
        for k in range(1, DP):
            total = total + grad_r[k - 1]
        grad_out[d_here, :] = total
        for k in range(1, DP):
            grad_gather(k).start()

    def update():
        for k in range(1, DP):
            grad_gather(k).wait_recv()
        new_a, a_one, a_two = apply_adam_step(
            a_ref[...], am_ref[...], av_ref[...], grad_out[:RANK, :]
        )
        a_out[...], am_out[...], av_out[...] = new_a, a_one, a_two
        high, low = two_terms(new_a)
        two_in[...] = dot_t(attn[...], jnp.concatenate([high, low], axis=0))
        sum_two.one()
        new_b, b_one, b_two = apply_adam_step(
            b_ref[...], bm_ref[...], bv_ref[...], grad_out[RANK:, :]
        )
        b_out[...], bm_out[...], bv_out[...] = new_b, b_one, b_two

    ways = [at(lax.rem(z + 1, ZN), y, c), at(lax.rem(z + ZN - 1, ZN), y, c)]

    def product(u, other_y, other_c):
        yy = (1 - y) if other_y else y
        cc = (1 - c) if other_c else c
        to = lax.rem(z + ZN + 4 + (1 - 2 * lax.rem(u, 2)) * ((u + 1) // 2), ZN)
        block = (to * 2 + yy) * 2 + cc
        cols = pl.ds(pl.multiple_of(block * FEAT, FEAT), FEAT)
        return dot(attn[...], w[:, cols])

    def core_copy(u):
        return remote(csend.at[u], crecv.at[u], c_s.at[u], c_r.at[u], core_peer)

    def y_copy(u):
        return remote(ysend.at[u], yrecv.at[u], y_s.at[u], y_r.at[u], y_peer)

    def core_stage(u):
        for k in range(2):
            csend[u, k] = product(u, k == 1, True)
        core_copy(u).start()

    def y_stage(u):
        own = product(u, False, False)
        other = product(u, True, False)
        core_copy(u).wait_recv()
        own = own + crecv[u, 0]
        other = other + crecv[u, 1]
        for half in range(2):
            low, mid, high = half * HALF, half * HALF + FIRST, (half + 1) * HALF
            ysend[u, half] = other[mid:high]
            zs[u, half, STREAMS[0], :] = other[low:mid]
            zs[u, half, STREAMS[1], :] = own[low:mid]
            zs[u, half, STREAMS[2], :] = own[mid:high]

    def y_add(u):
        y_copy(u).wait_recv()
        for half in range(2):
            zs[u, half, STREAMS[2], :] += yrecv[u, half]

    def unit(step, way):
        return 0 if step == 0 else 2 * step - 1 + way

    def z_copy(step, way, half, stream):
        return remote(
            zs.at[unit(step, way), half, STREAMS[stream]],
            zr.at[step, way, half, STREAMS[stream]],
            z_s.at[step, way, half, stream],
            z_r.at[step, way, half, stream],
            ways[way],
        )

    def z_send(step, stream, late):
        for way in range(2):
            half = way if late else 1 - way
            if step > 0 and (late or step > 1):
                z_copy(step - 1, way, half, stream).wait_recv()
                rows = STREAMS[stream]
                zs[unit(step, way), half, rows, :] += zr[step - 1, way, half, rows, :]
            z_copy(step, way, half, stream).start()

    def z_end(stream):
        rows = STREAMS[stream]
        for half in range(2):
            for way in range(2):
                z_copy(3, way, half, stream).wait_recv()
            zs[7, half, rows, :] += zr[3, 0, half, rows, :] + zr[3, 1, half, rows, :]

    def rest():
        sum_one.finish()
        for k in range(1, DP):
            grad_scatter(k).wait_send()
            grad_gather(k).wait_send()
        b_high, b_low = two_terms(b_out[...])
        right[...] = jnp.concatenate([b_high, b_high, b_high, b_high, b_low, b_low], axis=0)

    def base_sum():
        yfin_copy().wait_recv()
        for half in range(2):
            low, mid = half * HALF, half * HALF + FIRST
            base[pl.ds(low, FIRST), :] = zs[7, half, STREAMS[1], :] + yfin[half]
            base[pl.ds(mid, HALF - FIRST), :] = zs[7, half, STREAMS[2], :]

    def drain():
        yfin_copy().wait_send()
        for u in range(8):
            core_copy(u).wait_send()
            y_copy(u).wait_send()
        for way in range(2):
            for stream in range(3):
                z_copy(0, way, way, stream).wait_send()
                for after in range(1, 4):
                    for half in range(2):
                        z_copy(after, way, half, stream).wait_send()

    def yfin_copy():
        return remote(yfin_src, yfin, yf_s, yf_r, y_peer)

    attend = Attention(lengths, q, keys, values, fk, fv, attn, qs, sc, sn, mixed)
    for load in loads[4:8]:
        load.wait()
    sum_one.two()
    for load in loads[11:]:
        load.start()
    attend.scores()
    for load in loads[8:10]:
        load.wait()
    attend.mix()
    loads[10].wait()

    def next_units(u, carry):
        core_stage(u + 2)
        y_stage(u)
        return carry

    core_stage(0)
    core_stage(1)
    core_stage(2)
    y_stage(0)
    y_copy(0).start()
    z_send(0, 0, True)
    z_send(0, 1, True)
    sum_one.three()
    lax.fori_loop(1, 3, next_units, 0)
    y_copy(1).start()
    z_send(1, 0, False)
    z_send(1, 1, False)
    y_copy(2).start()
    y_add(0)
    z_send(0, 2, True)
    z_send(1, 0, True)
    z_send(1, 1, True)
    sum_one.four()
    gradients()
    lax.fori_loop(3, 5, next_units, 0)
    y_copy(3).start()
    y_copy(4).start()
    y_add(1)
    y_add(2)
    z_send(1, 2, False)
    z_send(1, 2, True)
    for load in loads[11:]:
        load.wait()
    z_send(2, 0, False)
    z_send(2, 0, True)
    z_send(2, 1, False)
    z_send(2, 1, True)
    gradient_sum()
    next_units(5, 0)
    y_copy(5).start()
    lax.fori_loop(6, 8, lambda u, carry: (y_stage(u), carry)[1], 0)
    y_copy(6).start()
    y_copy(7).start()
    y_add(3)
    y_add(4)
    z_send(2, 2, False)
    z_send(2, 2, True)
    update()
    sum_two.two()
    z_send(3, 0, False)
    z_send(3, 0, True)
    z_send(3, 1, False)
    z_send(3, 1, True)
    z_end(0)
    for half in range(2):
        yfin_src[half] = zs[7, half, STREAMS[0], :]
    yfin_copy().start()
    y_add(5)
    y_add(6)
    sum_two.three()
    z_send(3, 2, False)
    z_send(3, 2, True)
    rest()
    z_end(1)
    sum_two.four()
    y_add(7)
    z_end(2)
    base_sum()
    drain()
    sum_two.five()
    u_high, u_low = two_terms(two_out[...])
    left = jnp.concatenate([u_high, u_low, u_high], axis=1)
    dec[...] = (base[...] + adapter_scale * dot(left, right[...])).astype(BF16)
    sum_two.finish()


def step(*args):
    vmem = pl.BlockSpec(memory_space=pltpu.VMEM)
    factor = jax.ShapeDtypeStruct((RANK, FEAT), F32)
    dma = pltpu.SemaphoreType.DMA
    places = [pltpu.SMEM if arg.ndim == 1 else pltpu.VMEM for arg in args]
    small = [
        pltpu.VMEM((256, 128), F32),
        pltpu.VMEM((128, 128), F32),
        pltpu.VMEM((128, 128), F32),
        pltpu.VMEM((CHIPS - 1, 8, 128), F32),
        pltpu.VMEM((256, 128), F32),
    ]
    return pl.pallas_call(
        step_kernel,
        out_shape=(jax.ShapeDtypeStruct((ROWS, FEAT), BF16),) + (factor,) * 6,
        in_specs=[pl.BlockSpec(memory_space=pltpu.HBM)] * len(args),
        out_specs=(vmem,) * 7,
        scratch_shapes=[
            *[place(arg.shape, arg.dtype) for place, arg in zip(places, args)],
            pltpu.VMEM((ROWS, FEAT), BF16),
            pltpu.VMEM((ROWS, FEAT), F32),
            pltpu.VMEM((6 * RANK, FEAT), BF16),
            pltpu.VMEM((512, 128), BF16),
            pltpu.VMEM((512, 256), F32),
            pltpu.VMEM((512, 128), F32),
            pltpu.VMEM((512, 128), F32),
            pltpu.VMEM((8, 2, ROWS, FEAT), F32),
            pltpu.VMEM((8, 2, ROWS, FEAT), F32),
            pltpu.VMEM((8, 2, HALF - FIRST, FEAT), F32),
            pltpu.VMEM((8, 2, HALF - FIRST, FEAT), F32),
            pltpu.VMEM((8, 2, HALF + FIRST, FEAT), F32),
            pltpu.VMEM((4, 2, 2, HALF + FIRST, FEAT), F32),
            pltpu.VMEM((2, FIRST, FEAT), F32),
            pltpu.VMEM((2, FIRST, FEAT), F32),
            *small,
            pltpu.VMEM((128, FEAT), F32),
            pltpu.VMEM((7, 16, FEAT), F32),
            pltpu.VMEM((128, FEAT), F32),
            *small,
            dma((len(args),)),
            dma((8,)), dma((8,)), dma((8,)), dma((8,)),
            dma((4, 2, 2, 3)), dma((4, 2, 2, 3)),
            dma, dma,
            dma((78,)), dma((78,)),
        ],
        compiler_params=pltpu.CompilerParams(
            collective_id=0, has_side_effects=True, vmem_limit_bytes=52 * 1024 * 1024
        ),
    )(*[pltpu.with_memory_space_constraint(arg, pltpu.HBM) for arg in args])


def hand_out_kernel(*refs):
    half = len(refs) // 2
    copies = [
        pltpu.make_async_copy(src, dst, refs[-1].at[i])
        for i, (src, dst) in enumerate(zip(refs[:half], refs[half:-1]))
    ]
    for copy in copies:
        copy.start()
    for copy in copies:
        copy.wait()


def hand_out(*args):
    return pl.pallas_call(
        hand_out_kernel,
        out_shape=tuple(jax.ShapeDtypeStruct(arg.shape, arg.dtype) for arg in args),
        in_specs=[pl.BlockSpec(memory_space=pltpu.VMEM)] * len(args),
        out_specs=(pl.BlockSpec(memory_space=pltpu.HBM),) * len(args),
        scratch_shapes=[pltpu.SemaphoreType.DMA((len(args),))],
        compiler_params=pltpu.CompilerParams(vmem_limit_bytes=4 * 1024 * 1024),
    )(*args)


def per_device(
    projection_input,
    output_gradient,
    adapter_down,
    adapter_up,
    down_first_moment,
    down_second_moment,
    up_first_moment,
    up_second_moment,
    projection_weight,
    queries,
    stored_keys,
    stored_values,
    fresh_keys,
    fresh_values,
    lengths,
):
    results = step(
        projection_input,
        output_gradient,
        adapter_down.T,
        adapter_up,
        lengths,
        queries.reshape(ROWS, FEAT),
        fresh_keys.reshape(ROWS, 128),
        stored_keys,
        fresh_values.reshape(ROWS, 128),
        stored_values,
        projection_weight,
        down_first_moment.T,
        down_second_moment.T,
        up_first_moment,
        up_second_moment,
    )
    decoded, new_a, new_b, a_one, a_two, b_one, b_two = hand_out(*results)
    return (
        decoded.reshape(queries.shape), new_a.T, new_b, a_one.T, a_two.T, b_one, b_two
    )


def solution(mesh):
    return jax.shard_map(
        per_device,
        mesh=mesh,
        in_specs=(
            P("dp", "tensor"),
            P("dp", "tensor"),
            P("tensor", None),
            P(None, "tensor"),
            P("tensor", None),
            P("tensor", None),
            P(None, "tensor"),
            P(None, "tensor"),
            P("tensor", None),
            P(None, "dp", "tensor"),
            P("dp", None, "tensor"),
            P("dp", None, "tensor"),
            P(None, "dp", "tensor"),
            P(None, "dp", "tensor"),
            P("dp"),
        ),
        out_specs=(
            P(None, "dp", "tensor"),
            P("tensor", None),
            P(None, "tensor"),
            P("tensor", None),
            P("tensor", None),
            P(None, "tensor"),
            P(None, "tensor"),
        ),
        check_vma=False,
    )
```

```python
import functools
import math

import jax
import jax.numpy as jnp
from jax import lax
from jax.experimental import pallas as pl
from jax.experimental.pallas import tpu as pltpu
from jax.sharding import PartitionSpec as P

beta_one = 0.9
beta_two = 0.999
learn_rate = 0.005
adam_count = 10.0
adam_eps = 1e-08
adapter_scale = 2.0

F32 = jnp.float32
BF16 = jnp.bfloat16
MESH = pl.DeviceIdType.MESH

ROWS = 256
FEAT = 256
RANK = 64
ZN = 8
CHIPS = 16
DP = 8
HALF = ROWS // 2
FIRST = 64
STREAMS = (pl.ds(0, FIRST), pl.ds(FIRST, FIRST), pl.ds(2 * FIRST, HALF - FIRST))


def apply_adam_step(current, moment_one, moment_two, gradient):
    moment_one = beta_one * moment_one + (1.0 - beta_one) * gradient
    moment_two = beta_two * moment_two + (1.0 - beta_two) * gradient * gradient
    fix_one = 1.0 - beta_one**adam_count
    fix_two = 1.0 - beta_two**adam_count
    updated = current - learn_rate * (moment_one / fix_one) / (
        jnp.sqrt(moment_two / fix_two) + adam_eps
    )
    return (updated, moment_one, moment_two)


def dot(a, b):
    return jnp.dot(a, b, preferred_element_type=F32)


def dot_t(a, b):
    return lax.dot_general(a, b, (((1,), (1,)), ((), ())), preferred_element_type=F32)


def two_terms(a):
    high = a.astype(BF16)
    low = (a - high.astype(F32)).astype(BF16)
    return high, low


class Attention:
    def __init__(self, lengths, q, k, v, fk, fv, out, qs, sc, sn, mixed):
        self.lengths, self.q, self.k, self.v, self.fk, self.fv = lengths, q, k, v, fk, fv
        self.out, self.qs, self.sc, self.sn, self.mixed = out, qs, sc, sn, mixed
        self.pairs = k.shape[0] // 2
        i0 = lax.broadcasted_iota(jnp.int32, (ROWS, ROWS), 0)
        i1 = lax.broadcasted_iota(jnp.int32, (ROWS, ROWS), 1)
        self.perm = jnp.where(i1 == (i0 % 4) * 64 + i0 // 4, 1.0, 0.0).astype(BF16)
        self.back = jnp.where(i0 == (i1 % 4) * 64 + i1 // 4, 1.0, 0.0).astype(BF16)

    def scores(self):
        pairs, qs, sc, sn = self.pairs, self.qs, self.sc, self.sn
        inv_root = 1.0 / math.sqrt(128)
        qp = dot(self.perm, self.q[...])
        qp = jnp.concatenate(
            [qp[:, :128].reshape(pairs, 8, 128), qp[:, 128:].reshape(pairs, 8, 128)], axis=1
        )
        qs[...] = qp.reshape(pairs * 16, 128).astype(BF16)
        fk = dot(self.perm, self.fk[...]).astype(BF16)

        row = lax.broadcasted_iota(jnp.int32, (16, 256), 0)
        col = lax.broadcasted_iota(jnp.int32, (16, 256), 1)
        second = (row // 4) % 2 == 1
        start = jnp.where(second, 128, 0)

        def one_pair(p, carry):
            keys = self.k[pl.ds(2 * p, 2)].reshape(256, 128)
            at = pl.ds(pl.multiple_of(p * 16, 16), 16)
            s = dot_t(qs[at, :], keys) * inv_root
            stop = jnp.where(second, 128 + self.lengths[2 * p + 1], self.lengths[2 * p])
            sc[at, :] = jnp.where((col >= start) & (col < stop), s, -jnp.inf)
            return carry

        lax.fori_loop(0, pairs, one_pair, 0, unroll=32)

        nrow = lax.broadcasted_iota(jnp.int32, (256, 128), 0)
        ncol = lax.broadcasted_iota(jnp.int32, (256, 128), 1)
        request = (nrow // 16) * 2 + (nrow // 4) % 2
        new_live = (ncol // 4 == request) & (ncol % 4 <= nrow % 4)
        for half in range(2):
            part = pl.ds(half * 256, 256)
            s = dot_t(qs[part, :], fk[half * 128 : half * 128 + 128]) * inv_root
            sn[part, :] = jnp.where(new_live, s, -jnp.inf)

    def mix(self):
        sc, sn, mixed = self.sc, self.sn, self.mixed
        pairs = self.pairs
        fv = dot(self.perm, self.fv[...]).astype(BF16)
        for block in range(8):
            part = pl.ds(block * 64, 64)
            s, n = sc[part, :], sn[part, :]
            largest = jnp.maximum(
                jnp.max(s, axis=1, keepdims=True), jnp.max(n, axis=1, keepdims=True)
            )
            e, m = jnp.exp(s - largest), jnp.exp(n - largest)
            total = jnp.sum(e, axis=1, keepdims=True) + jnp.sum(m, axis=1, keepdims=True)
            scale = 1.0 / total
            weights = (e * scale).astype(BF16)
            where_new = (block // 4) * 128
            new = dot((m * scale).astype(BF16), fv[where_new : where_new + 128])
            for i in range(4):
                p = block * 4 + i
                values = self.v[2 * p : 2 * p + 2].reshape(256, 128)
                mixed[p * 16 : p * 16 + 16, :] = (
                    dot(weights[i * 16 : i * 16 + 16], values) + new[i * 16 : i * 16 + 16]
                )
        o = mixed[...].reshape(pairs, 16, 128)
        o = jnp.concatenate(
            [o[:, :8].reshape(ROWS, 128), o[:, 8:].reshape(ROWS, 128)], axis=1
        ).astype(BF16)
        self.out[...] = dot(self.back, o).astype(BF16)


def step_kernel(
    x_h, dy_h, a_h, b_h, len_h, q_h, fk_h, k_h, fv_h, v_h, w_h, am_h, av_h, bm_h, bv_h,
    dec, a_out, b_out, am_out, av_out, bm_out, bv_out,
    x, dy, a_ref, b_ref, lengths, q, fk, keys, fv, values, w, am_ref, av_ref, bm_ref, bv_ref,
    attn, base, right, qs, sc, sn, mixed,
    csend, crecv, ysend, yrecv, zs, zr, yfin_src, yfin,
    one_in, one_core, one_half, one_recv, one_out,
    grad, grad_r, grad_out,
    two_in, two_core, two_half, two_recv, two_out,
    in_sem, c_s, c_r, y_s, y_r, z_s, z_r, yf_s, yf_r, t_s, t_r,
):
    d = lax.axis_index("dp")
    t = lax.axis_index("tensor")
    z, y, c = t // 4, (t // 2) % 2, t % 2

    def at(zz, yy, cc):
        return (d, (zz * 2 + yy) * 2 + cc)

    core_peer = at(z, y, 1 - c)
    y_peer = at(z, 1 - y, c)
    chip = z * 2 + y
    chip_peers = [(d, lax.rem(chip + k, CHIPS) * 2 + c) for k in range(1, CHIPS)]
    dp_peers = [(lax.rem(d + k, DP), t) for k in range(1, DP)]

    barrier = pltpu.get_barrier_semaphore()
    everyone = chip_peers[7:] + chip_peers[:7][::-1] + dp_peers + [core_peer]
    for peer in everyone:
        pl.semaphore_signal(barrier, inc=1, device_id=peer, device_id_type=MESH)

    here = (x, dy, a_ref, b_ref, lengths, q, fk, keys, fv, values, w, am_ref, av_ref, bm_ref, bv_ref)
    there = (x_h, dy_h, a_h, b_h, len_h, q_h, fk_h, k_h, fv_h, v_h, w_h, am_h, av_h, bm_h, bv_h)
    loads = [
        pltpu.make_async_copy(src, dst, in_sem.at[i])
        for i, (src, dst) in enumerate(zip(there, here))
    ]
    for load in loads[:8]:
        load.start()

    def remote(src, dst, send_sem, recv_sem, peer):
        return pltpu.make_async_remote_copy(
            src_ref=src,
            dst_ref=dst,
            send_sem=send_sem,
            recv_sem=recv_sem,
            device_id=peer,
            device_id_type=MESH,
        )

    class TensorSum:
        def __init__(self, src, core_recv, half, recv, out, first, pairs):
            self.src, self.core_recv, self.half = src, core_recv, half
            self.recv, self.out, self.first, self.pairs = recv, out, first, pairs
            rows = half.shape[0]
            part = z if pairs else chip
            self.mine = pl.ds(pl.multiple_of(c * rows, rows), rows)
            self.theirs = pl.ds(pl.multiple_of((1 - c) * rows, rows), rows)
            self.part = pl.ds(pl.multiple_of(part * 8, 8), 8)
            self.here = pl.ds(pl.multiple_of(c * rows + part * 8, 8), 8)
            self.back = range(2, CHIPS, 2) if pairs else range(1, CHIPS)

        def core_scatter(self):
            i = self.first
            return remote(self.src.at[self.theirs], self.core_recv, t_s.at[i], t_r.at[i], core_peer)

        def scatter(self, k):
            to = lax.rem(chip + k, CHIPS)
            part = pl.ds(pl.multiple_of((to // 2 if self.pairs else to) * 8, 8), 8)
            i = self.first + k
            return remote(
                self.half.at[part], self.recv.at[k - 1], t_s.at[i], t_r.at[i], chip_peers[k - 1]
            )

        def gather(self, k):
            i = self.first + 15 + k
            return remote(
                self.out.at[self.here], self.out.at[self.here],
                t_s.at[i], t_r.at[i], chip_peers[k - 1],
            )

        def core_gather(self):
            i = self.first + 31
            return remote(
                self.out.at[self.mine], self.out.at[self.mine], t_s.at[i], t_r.at[i], core_peer
            )

        def one(self):
            self.core_scatter().start()

        def two(self):
            self.core_scatter().wait_recv()
            self.half[...] = self.src[self.mine, :] + self.core_recv[...]
            for k in range(1, CHIPS):
                self.scatter(k).start()

        def three(self):
            for k in range(1, CHIPS):
                self.scatter(k).wait_recv()
            total = self.half[self.part, :]
            for k in range(1, CHIPS):
                total = total + self.recv[k - 1]
            self.out[self.here, :] = total
            for k in self.back:
                self.gather(k).start()

        def four(self):
            for k in self.back:
                self.gather(k).wait_recv()
            self.core_gather().start()

        def five(self):
            self.core_gather().wait_recv()

        def finish(self):
            self.core_scatter().wait_send()
            self.core_gather().wait_send()
            for k in range(1, CHIPS):
                self.scatter(k).wait_send()
            for k in self.back:
                self.gather(k).wait_send()

    sum_one = TensorSum(one_in, one_core, one_half, one_recv, one_out, 0, False)
    sum_two = TensorSum(two_in, two_core, two_half, two_recv, two_out, 32, True)

    for load in loads[:4]:
        load.wait()
    for load in loads[8:11]:
        load.start()
    a_high, a_low = two_terms(a_ref[...])
    b_high, b_low = two_terms(b_ref[...])
    one_in[...] = jnp.concatenate(
        [
            dot_t(x[...], a_high) + dot_t(x[...], a_low),
            dot_t(dy[...], b_high) + dot_t(dy[...], b_low),
        ],
        axis=1,
    )
    pl.semaphore_wait(barrier, len(everyone))
    sum_one.one()

    d_here = pl.ds(pl.multiple_of(d * 16, 16), 16)

    def grad_scatter(k):
        part = pl.ds(pl.multiple_of(lax.rem(d + k, DP) * 16, 16), 16)
        i = 64 + k - 1
        return remote(grad.at[part], grad_r.at[k - 1], t_s.at[i], t_r.at[i], dp_peers[k - 1])

    def grad_gather(k):
        i = 71 + k - 1
        return remote(
            grad_out.at[d_here], grad_out.at[d_here], t_s.at[i], t_r.at[i], dp_peers[k - 1]
        )

    def gradients():
        sum_one.five()
        scale = adapter_scale / (ROWS * DP)
        both = one_out[...].T
        x_high, x_low = two_terms(both[:RANK])
        g_high, g_low = two_terms(both[RANK:])
        grad[:RANK, :] = scale * (dot(g_high, x[...]) + dot(g_low, x[...]))
        grad[RANK:, :] = scale * (dot(x_high, dy[...]) + dot(x_low, dy[...]))
        for k in range(1, DP):
            grad_scatter(k).start()

    def gradient_sum():
        for k in range(1, DP):
            grad_scatter(k).wait_recv()
        total = grad[d_here, :]
        for k in range(1, DP):
            total = total + grad_r[k - 1]
        grad_out[d_here, :] = total
        for k in range(1, DP):
            grad_gather(k).start()

    def update():
        for k in range(1, DP):
            grad_gather(k).wait_recv()
        new_a, a_one, a_two = apply_adam_step(
            a_ref[...], am_ref[...], av_ref[...], grad_out[:RANK, :]
        )
        a_out[...], am_out[...], av_out[...] = new_a, a_one, a_two
        high, low = two_terms(new_a)
        none = jnp.zeros_like(high)
        first, second = attn[:HALF, :], attn[HALF:, :]
        two_in[...] = (
            dot_t(first, jnp.concatenate([high, none], axis=0))
            + dot_t(second, jnp.concatenate([none, high], axis=0))
        ) + (
            dot_t(first, jnp.concatenate([low, none], axis=0))
            + dot_t(second, jnp.concatenate([none, low], axis=0))
        )
        sum_two.one()
        new_b, b_one, b_two = apply_adam_step(
            b_ref[...], bm_ref[...], bv_ref[...], grad_out[RANK:, :]
        )
        b_out[...], bm_out[...], bv_out[...] = new_b, b_one, b_two

    ways = [at(lax.rem(z + 1, ZN), y, c), at(lax.rem(z + ZN - 1, ZN), y, c)]

    def product(u, other_y, other_c):
        yy = (1 - y) if other_y else y
        cc = (1 - c) if other_c else c
        to = lax.rem(z + ZN + 4 + (1 - 2 * lax.rem(u, 2)) * ((u + 1) // 2), ZN)
        block = (to * 2 + yy) * 2 + cc
        cols = pl.ds(pl.multiple_of(block * FEAT, FEAT), FEAT)
        return dot(attn[...], w[:, cols])

    def core_copy(u):
        return remote(csend.at[u], crecv.at[u], c_s.at[u], c_r.at[u], core_peer)

    def y_copy(u):
        return remote(ysend.at[u], yrecv.at[u], y_s.at[u], y_r.at[u], y_peer)

    def core_stage(u):
        for k in range(2):
            csend[u, k] = product(u, k == 1, True)
        core_copy(u).start()

    def y_stage(u):
        own = product(u, False, False)
        other = product(u, True, False)
        core_copy(u).wait_recv()
        own = own + crecv[u, 0]
        other = other + crecv[u, 1]
        for half in range(2):
            low, mid, high = half * HALF, half * HALF + FIRST, (half + 1) * HALF
            ysend[u, half] = other[mid:high]
            zs[u, half, STREAMS[0], :] = other[low:mid]
            zs[u, half, STREAMS[1], :] = own[low:mid]
            zs[u, half, STREAMS[2], :] = own[mid:high]

    def y_add(u):
        y_copy(u).wait_recv()
        for half in range(2):
            zs[u, half, STREAMS[2], :] += yrecv[u, half]

    def unit(step, way):
        return 0 if step == 0 else 2 * step - 1 + way

    def z_copy(step, way, half, stream):
        return remote(
            zs.at[unit(step, way), half, STREAMS[stream]],
            zr.at[step, way, half, STREAMS[stream]],
            z_s.at[step, way, half, stream],
            z_r.at[step, way, half, stream],
            ways[way],
        )

    def z_send(step, stream, late):
        for way in range(2):
            half = way if late else 1 - way
            if step > 0 and (late or step > 1):
                z_copy(step - 1, way, half, stream).wait_recv()
                rows = STREAMS[stream]
                zs[unit(step, way), half, rows, :] += zr[step - 1, way, half, rows, :]
            z_copy(step, way, half, stream).start()

    def z_end(stream):
        rows = STREAMS[stream]
        for half in range(2):
            for way in range(2):
                z_copy(3, way, half, stream).wait_recv()
            zs[7, half, rows, :] += zr[3, 0, half, rows, :] + zr[3, 1, half, rows, :]

    def rest():
        sum_one.finish()
        for k in range(1, DP):
            grad_scatter(k).wait_send()
            grad_gather(k).wait_send()
        b_high, b_low = two_terms(b_out[...])
        none = jnp.zeros_like(b_high)
        right[0] = jnp.concatenate([b_high, none, b_high, none, b_low, none], axis=0)
        right[1] = jnp.concatenate([none, b_high, none, b_high, none, b_low], axis=0)

    def base_sum():
        yfin_copy().wait_recv()
        for half in range(2):
            low, mid = half * HALF, half * HALF + FIRST
            base[pl.ds(low, FIRST), :] = zs[7, half, STREAMS[1], :] + yfin[half]
            base[pl.ds(mid, HALF - FIRST), :] = zs[7, half, STREAMS[2], :]

    def drain():
        yfin_copy().wait_send()
        for u in range(8):
            core_copy(u).wait_send()
            y_copy(u).wait_send()
        for way in range(2):
            for stream in range(3):
                z_copy(0, way, way, stream).wait_send()
                for after in range(1, 4):
                    for half in range(2):
                        z_copy(after, way, half, stream).wait_send()

    def yfin_copy():
        return remote(yfin_src, yfin, yf_s, yf_r, y_peer)

    attend = Attention(lengths, q, keys, values, fk, fv, attn, qs, sc, sn, mixed)
    for load in loads[4:8]:
        load.wait()
    sum_one.two()
    for load in loads[11:]:
        load.start()
    attend.scores()
    for load in loads[8:10]:
        load.wait()
    attend.mix()
    loads[10].wait()

    def next_units(u, carry):
        core_stage(u + 2)
        y_stage(u)
        return carry

    core_stage(0)
    core_stage(1)
    core_stage(2)
    y_stage(0)
    y_copy(0).start()
    z_send(0, 0, True)
    z_send(0, 1, True)
    sum_one.three()
    lax.fori_loop(1, 3, next_units, 0)
    y_copy(1).start()
    z_send(1, 0, False)
    z_send(1, 1, False)
    y_copy(2).start()
    y_add(0)
    z_send(0, 2, True)
    z_send(1, 0, True)
    z_send(1, 1, True)
    sum_one.four()
    gradients()
    lax.fori_loop(3, 5, next_units, 0)
    y_copy(3).start()
    y_copy(4).start()
    y_add(1)
    y_add(2)
    z_send(1, 2, False)
    z_send(1, 2, True)
    for load in loads[11:]:
        load.wait()
    z_send(2, 0, False)
    z_send(2, 0, True)
    z_send(2, 1, False)
    z_send(2, 1, True)
    gradient_sum()
    next_units(5, 0)
    y_copy(5).start()
    y_add(3)
    y_add(4)
    z_send(2, 2, False)
    z_send(2, 2, True)
    update()
    lax.fori_loop(6, 8, lambda u, carry: (y_stage(u), carry)[1], 0)
    y_copy(6).start()
    y_copy(7).start()
    sum_two.two()
    z_send(3, 0, False)
    z_send(3, 0, True)
    z_send(3, 1, False)
    z_send(3, 1, True)
    sum_two.three()
    z_end(0)
    for half in range(2):
        yfin_src[half] = zs[7, half, STREAMS[0], :]
    yfin_copy().start()
    y_add(5)
    y_add(6)
    z_send(3, 2, False)
    z_send(3, 2, True)
    rest()
    sum_two.four()
    z_end(1)
    y_add(7)
    z_end(2)
    base_sum()
    drain()
    sum_two.five()
    u_high, u_low = two_terms(two_out[...])
    left = jnp.concatenate([u_high, u_low, u_high], axis=1)
    for half in range(2):
        rows = pl.ds(half * HALF, HALF)
        dec[rows, :] = (base[rows, :] + adapter_scale * dot(left, right[half])).astype(BF16)
    sum_two.finish()


def step(*args):
    vmem = pl.BlockSpec(memory_space=pltpu.VMEM)
    factor = jax.ShapeDtypeStruct((RANK, FEAT), F32)
    dma = pltpu.SemaphoreType.DMA
    places = [pltpu.SMEM if arg.ndim == 1 else pltpu.VMEM for arg in args]
    small = [
        pltpu.VMEM((256, 128), F32),
        pltpu.VMEM((128, 128), F32),
        pltpu.VMEM((128, 128), F32),
        pltpu.VMEM((CHIPS - 1, 8, 128), F32),
        pltpu.VMEM((256, 128), F32),
    ]
    return pl.pallas_call(
        step_kernel,
        out_shape=(jax.ShapeDtypeStruct((ROWS, FEAT), BF16),) + (factor,) * 6,
        in_specs=[pl.BlockSpec(memory_space=pltpu.HBM)] * len(args),
        out_specs=(vmem,) * 7,
        scratch_shapes=[
            *[place(arg.shape, arg.dtype) for place, arg in zip(places, args)],
            pltpu.VMEM((ROWS, FEAT), BF16),
            pltpu.VMEM((ROWS, FEAT), F32),
            pltpu.VMEM((2, 6 * RANK, FEAT), BF16),
            pltpu.VMEM((512, 128), BF16),
            pltpu.VMEM((512, 256), F32),
            pltpu.VMEM((512, 128), F32),
            pltpu.VMEM((512, 128), F32),
            pltpu.VMEM((8, 2, ROWS, FEAT), F32),
            pltpu.VMEM((8, 2, ROWS, FEAT), F32),
            pltpu.VMEM((8, 2, HALF - FIRST, FEAT), F32),
            pltpu.VMEM((8, 2, HALF - FIRST, FEAT), F32),
            pltpu.VMEM((8, 2, HALF + FIRST, FEAT), F32),
            pltpu.VMEM((4, 2, 2, HALF + FIRST, FEAT), F32),
            pltpu.VMEM((2, FIRST, FEAT), F32),
            pltpu.VMEM((2, FIRST, FEAT), F32),
            *small,
            pltpu.VMEM((128, FEAT), F32),
            pltpu.VMEM((7, 16, FEAT), F32),
            pltpu.VMEM((128, FEAT), F32),
            pltpu.VMEM((128, 128), F32),
            pltpu.VMEM((64, 128), F32),
            pltpu.VMEM((64, 128), F32),
            pltpu.VMEM((CHIPS - 1, 8, 128), F32),
            pltpu.VMEM((128, 128), F32),
            dma((len(args),)),
            dma((8,)), dma((8,)), dma((8,)), dma((8,)),
            dma((4, 2, 2, 3)), dma((4, 2, 2, 3)),
            dma, dma,
            dma((78,)), dma((78,)),
        ],
        compiler_params=pltpu.CompilerParams(
            collective_id=0, has_side_effects=True, vmem_limit_bytes=52 * 1024 * 1024
        ),
    )(*[pltpu.with_memory_space_constraint(arg, pltpu.HBM) for arg in args])


def hand_out_kernel(*refs):
    half = len(refs) // 2
    copies = [
        pltpu.make_async_copy(src, dst, refs[-1].at[i])
        for i, (src, dst) in enumerate(zip(refs[:half], refs[half:-1]))
    ]
    for copy in copies:
        copy.start()
    for copy in copies:
        copy.wait()


def hand_out(*args):
    return pl.pallas_call(
        hand_out_kernel,
        out_shape=tuple(jax.ShapeDtypeStruct(arg.shape, arg.dtype) for arg in args),
        in_specs=[pl.BlockSpec(memory_space=pltpu.VMEM)] * len(args),
        out_specs=(pl.BlockSpec(memory_space=pltpu.HBM),) * len(args),
        scratch_shapes=[pltpu.SemaphoreType.DMA((len(args),))],
        compiler_params=pltpu.CompilerParams(vmem_limit_bytes=4 * 1024 * 1024),
    )(*args)


def per_device(
    projection_input,
    output_gradient,
    adapter_down,
    adapter_up,
    down_first_moment,
    down_second_moment,
    up_first_moment,
    up_second_moment,
    projection_weight,
    queries,
    stored_keys,
    stored_values,
    fresh_keys,
    fresh_values,
    lengths,
):
    results = step(
        projection_input,
        output_gradient,
        adapter_down.T,
        adapter_up,
        lengths,
        queries.reshape(ROWS, FEAT),
        fresh_keys.reshape(ROWS, 128),
        stored_keys,
        fresh_values.reshape(ROWS, 128),
        stored_values,
        projection_weight,
        down_first_moment.T,
        down_second_moment.T,
        up_first_moment,
        up_second_moment,
    )
    decoded, new_a, new_b, a_one, a_two, b_one, b_two = hand_out(*results)
    return (
        decoded.reshape(queries.shape), new_a.T, new_b, a_one.T, a_two.T, b_one, b_two
    )


def solution(mesh):
    return jax.shard_map(
        per_device,
        mesh=mesh,
        in_specs=(
            P("dp", "tensor"),
            P("dp", "tensor"),
            P("tensor", None),
            P(None, "tensor"),
            P("tensor", None),
            P("tensor", None),
            P(None, "tensor"),
            P(None, "tensor"),
            P("tensor", None),
            P(None, "dp", "tensor"),
            P("dp", None, "tensor"),
            P("dp", None, "tensor"),
            P(None, "dp", "tensor"),
            P(None, "dp", "tensor"),
            P("dp"),
        ),
        out_specs=(
            P(None, "dp", "tensor"),
            P("tensor", None),
            P(None, "tensor"),
            P("tensor", None),
            P("tensor", None),
            P(None, "tensor"),
            P(None, "tensor"),
        ),
        check_vma=False,
    )
```

```python
import functools
import math

import jax
import jax.numpy as jnp
from jax import lax
from jax.experimental import pallas as pl
from jax.experimental.pallas import tpu as pltpu
from jax.sharding import PartitionSpec as P

beta_one = 0.9
beta_two = 0.999
learn_rate = 0.005
adam_count = 10.0
adam_eps = 1e-08
adapter_scale = 2.0

F32 = jnp.float32
BF16 = jnp.bfloat16
MESH = pl.DeviceIdType.MESH

ROWS = 256
FEAT = 256
RANK = 64
ZN = 8
CHIPS = 16
DP = 8
HALF = ROWS // 2
FIRST = 64
STREAMS = (pl.ds(0, FIRST), pl.ds(FIRST, FIRST), pl.ds(2 * FIRST, HALF - FIRST))


def apply_adam_step(current, moment_one, moment_two, gradient):
    moment_one = beta_one * moment_one + (1.0 - beta_one) * gradient
    moment_two = beta_two * moment_two + (1.0 - beta_two) * gradient * gradient
    fix_one = 1.0 - beta_one**adam_count
    fix_two = 1.0 - beta_two**adam_count
    updated = current - learn_rate * (moment_one / fix_one) / (
        jnp.sqrt(moment_two / fix_two) + adam_eps
    )
    return (updated, moment_one, moment_two)


def dot(a, b):
    return jnp.dot(a, b, preferred_element_type=F32)


def dot_t(a, b):
    return lax.dot_general(a, b, (((1,), (1,)), ((), ())), preferred_element_type=F32)


def two_terms(a):
    high = a.astype(BF16)
    low = (a - high.astype(F32)).astype(BF16)
    return high, low


class Attention:
    def __init__(self, lengths, q, k, v, fk, fv, out, qs, sc, sn, mixed):
        self.lengths, self.q, self.k, self.v, self.fk, self.fv = lengths, q, k, v, fk, fv
        self.out, self.qs, self.sc, self.sn, self.mixed = out, qs, sc, sn, mixed
        self.pairs = k.shape[0] // 2
        i0 = lax.broadcasted_iota(jnp.int32, (ROWS, ROWS), 0)
        i1 = lax.broadcasted_iota(jnp.int32, (ROWS, ROWS), 1)
        self.perm = jnp.where(i1 == (i0 % 4) * 64 + i0 // 4, 1.0, 0.0).astype(BF16)
        self.back = jnp.where(i0 == (i1 % 4) * 64 + i1 // 4, 1.0, 0.0).astype(BF16)

    def scores(self):
        pairs, qs, sc, sn = self.pairs, self.qs, self.sc, self.sn
        inv_root = 1.0 / math.sqrt(128)
        qp = dot(self.perm, self.q[...])
        qp = jnp.concatenate(
            [qp[:, :128].reshape(pairs, 8, 128), qp[:, 128:].reshape(pairs, 8, 128)], axis=1
        )
        qs[...] = qp.reshape(pairs * 16, 128).astype(BF16)
        fk = dot(self.perm, self.fk[...]).astype(BF16)

        row = lax.broadcasted_iota(jnp.int32, (16, 256), 0)
        col = lax.broadcasted_iota(jnp.int32, (16, 256), 1)
        second = (row // 4) % 2 == 1
        start = jnp.where(second, 128, 0)

        def one_pair(p, carry):
            keys = self.k[pl.ds(2 * p, 2)].reshape(256, 128)
            at = pl.ds(pl.multiple_of(p * 16, 16), 16)
            s = dot_t(qs[at, :], keys) * inv_root
            stop = jnp.where(second, 128 + self.lengths[2 * p + 1], self.lengths[2 * p])
            sc[at, :] = jnp.where((col >= start) & (col < stop), s, -jnp.inf)
            return carry

        lax.fori_loop(0, pairs, one_pair, 0, unroll=32)

        nrow = lax.broadcasted_iota(jnp.int32, (256, 128), 0)
        ncol = lax.broadcasted_iota(jnp.int32, (256, 128), 1)
        request = (nrow // 16) * 2 + (nrow // 4) % 2
        new_live = (ncol // 4 == request) & (ncol % 4 <= nrow % 4)
        for half in range(2):
            part = pl.ds(half * 256, 256)
            s = dot_t(qs[part, :], fk[half * 128 : half * 128 + 128]) * inv_root
            sn[part, :] = jnp.where(new_live, s, -jnp.inf)

    def mix(self):
        sc, sn, mixed = self.sc, self.sn, self.mixed
        pairs = self.pairs
        fv = dot(self.perm, self.fv[...]).astype(BF16)
        for block in range(8):
            part = pl.ds(block * 64, 64)
            s, n = sc[part, :], sn[part, :]
            largest = jnp.maximum(
                jnp.max(s, axis=1, keepdims=True), jnp.max(n, axis=1, keepdims=True)
            )
            e, m = jnp.exp(s - largest), jnp.exp(n - largest)
            total = jnp.sum(e, axis=1, keepdims=True) + jnp.sum(m, axis=1, keepdims=True)
            scale = 1.0 / total
            weights = (e * scale).astype(BF16)
            where_new = (block // 4) * 128
            new = dot((m * scale).astype(BF16), fv[where_new : where_new + 128])
            for i in range(4):
                p = block * 4 + i
                values = self.v[2 * p : 2 * p + 2].reshape(256, 128)
                mixed[p * 16 : p * 16 + 16, :] = (
                    dot(weights[i * 16 : i * 16 + 16], values) + new[i * 16 : i * 16 + 16]
                )
        o = mixed[...].reshape(pairs, 16, 128)
        o = jnp.concatenate(
            [o[:, :8].reshape(ROWS, 128), o[:, 8:].reshape(ROWS, 128)], axis=1
        ).astype(BF16)
        self.out[...] = dot(self.back, o).astype(BF16)


def step_kernel(
    x_h, dy_h, a_h, b_h, len_h, q_h, fk_h, k_h, fv_h, v_h, w_h, am_h, av_h, bm_h, bv_h,
    dec, a_out, b_out, am_out, av_out, bm_out, bv_out,
    x, dy, a_ref, b_ref, lengths, q, fk, keys, fv, values, w, am_ref, av_ref, bm_ref, bv_ref,
    attn, base, right, qs, sc, sn, mixed,
    csend, crecv, ysend, yrecv, zs, zr, yfin_src, yfin,
    one_in, one_core, one_half, one_recv, one_out,
    grad, grad_r, grad_out,
    two_in, two_core, two_half, two_recv, two_out,
    in_sem, c_s, c_r, y_s, y_r, z_s, z_r, yf_s, yf_r, t_s, t_r,
):
    d = lax.axis_index("dp")
    t = lax.axis_index("tensor")
    z, y, c = t // 4, (t // 2) % 2, t % 2

    def at(zz, yy, cc):
        return (d, (zz * 2 + yy) * 2 + cc)

    core_peer = at(z, y, 1 - c)
    y_peer = at(z, 1 - y, c)
    chip = z * 2 + y
    chip_peers = [(d, lax.rem(chip + k, CHIPS) * 2 + c) for k in range(1, CHIPS)]
    dp_peers = [(lax.rem(d + k, DP), t) for k in range(1, DP)]

    barrier = pltpu.get_barrier_semaphore()
    everyone = chip_peers[7:] + chip_peers[:7][::-1] + dp_peers + [core_peer]
    for peer in everyone:
        pl.semaphore_signal(barrier, inc=1, device_id=peer, device_id_type=MESH)

    here = (x, dy, a_ref, b_ref, lengths, q, fk, keys, fv, values, w, am_ref, av_ref, bm_ref, bv_ref)
    there = (x_h, dy_h, a_h, b_h, len_h, q_h, fk_h, k_h, fv_h, v_h, w_h, am_h, av_h, bm_h, bv_h)
    loads = [
        pltpu.make_async_copy(src, dst, in_sem.at[i])
        for i, (src, dst) in enumerate(zip(there, here))
    ]
    for load in loads[:8]:
        load.start()

    def remote(src, dst, send_sem, recv_sem, peer):
        return pltpu.make_async_remote_copy(
            src_ref=src,
            dst_ref=dst,
            send_sem=send_sem,
            recv_sem=recv_sem,
            device_id=peer,
            device_id_type=MESH,
        )

    class TensorSum:
        def __init__(self, src, core_recv, half, recv, out, first, pairs):
            self.src, self.core_recv, self.half = src, core_recv, half
            self.recv, self.out, self.first, self.pairs = recv, out, first, pairs
            rows = half.shape[0]
            size = recv.shape[1]
            part = z if pairs else chip
            self.mine = pl.ds(pl.multiple_of(c * rows, rows), rows)
            self.theirs = pl.ds(pl.multiple_of((1 - c) * rows, rows), rows)
            self.size = size
            self.part = pl.ds(pl.multiple_of(part * size, size), size)
            self.here = pl.ds(pl.multiple_of(c * rows + part * size, size), size)
            self.back = range(2, CHIPS, 2) if pairs else range(1, CHIPS)

        def core_scatter(self):
            i = self.first
            return remote(self.src.at[self.theirs], self.core_recv, t_s.at[i], t_r.at[i], core_peer)

        def scatter(self, k):
            to = lax.rem(chip + k, CHIPS)
            size = self.size
            part = pl.ds(pl.multiple_of((to // 2 if self.pairs else to) * size, size), size)
            i = self.first + k
            return remote(
                self.half.at[part], self.recv.at[k - 1], t_s.at[i], t_r.at[i], chip_peers[k - 1]
            )

        def gather(self, k):
            i = self.first + 15 + k
            return remote(
                self.out.at[self.here], self.out.at[self.here],
                t_s.at[i], t_r.at[i], chip_peers[k - 1],
            )

        def core_gather(self):
            i = self.first + 31
            return remote(
                self.out.at[self.mine], self.out.at[self.mine], t_s.at[i], t_r.at[i], core_peer
            )

        def one(self):
            self.core_scatter().start()

        def two(self):
            self.core_scatter().wait_recv()
            self.half[...] = self.src[self.mine, :] + self.core_recv[...]
            for k in range(1, CHIPS):
                self.scatter(k).start()

        def three(self):
            for k in range(1, CHIPS):
                self.scatter(k).wait_recv()
            total = self.half[self.part, :]
            for k in range(1, CHIPS):
                total = total + self.recv[k - 1]
            self.out[self.here, :] = total
            for k in self.back:
                self.gather(k).start()

        def four(self):
            for k in self.back:
                self.gather(k).wait_recv()
            self.core_gather().start()

        def five(self):
            self.core_gather().wait_recv()

        def finish(self):
            self.core_scatter().wait_send()
            self.core_gather().wait_send()
            for k in range(1, CHIPS):
                self.scatter(k).wait_send()
            for k in self.back:
                self.gather(k).wait_send()

    sum_one = TensorSum(one_in, one_core, one_half, one_recv, one_out, 0, True)
    sum_two = TensorSum(two_in, two_core, two_half, two_recv, two_out, 32, True)

    for load in loads[:4]:
        load.wait()
    for load in loads[8:11]:
        load.start()
    a_high, a_low = two_terms(a_ref[...])
    b_high, b_low = two_terms(b_ref[...])
    one_in[...] = jnp.concatenate(
        [
            dot_t(x[...], a_high) + dot_t(x[...], a_low),
            dot_t(dy[...], b_high) + dot_t(dy[...], b_low),
        ],
        axis=1,
    )
    pl.semaphore_wait(barrier, len(everyone))
    sum_one.one()

    d_here = pl.ds(pl.multiple_of(d * 16, 16), 16)

    def grad_scatter(k):
        part = pl.ds(pl.multiple_of(lax.rem(d + k, DP) * 16, 16), 16)
        i = 64 + k - 1
        return remote(grad.at[part], grad_r.at[k - 1], t_s.at[i], t_r.at[i], dp_peers[k - 1])

    def grad_gather(k):
        i = 71 + k - 1
        return remote(
            grad_out.at[d_here], grad_out.at[d_here], t_s.at[i], t_r.at[i], dp_peers[k - 1]
        )

    def gradients():
        sum_one.five()
        scale = adapter_scale / (ROWS * DP)
        both = one_out[...].T
        x_high, x_low = two_terms(both[:RANK])
        g_high, g_low = two_terms(both[RANK:])
        grad[:RANK, :] = scale * (dot(g_high, x[...]) + dot(g_low, x[...]))
        grad[RANK:, :] = scale * (dot(x_high, dy[...]) + dot(x_low, dy[...]))
        for k in range(1, DP):
            grad_scatter(k).start()

    def gradient_sum():
        for k in range(1, DP):
            grad_scatter(k).wait_recv()
        total = grad[d_here, :]
        for k in range(1, DP):
            total = total + grad_r[k - 1]
        grad_out[d_here, :] = total
        for k in range(1, DP):
            grad_gather(k).start()

    def update():
        for k in range(1, DP):
            grad_gather(k).wait_recv()
        new_a, a_one, a_two = apply_adam_step(
            a_ref[...], am_ref[...], av_ref[...], grad_out[:RANK, :]
        )
        a_out[...], am_out[...], av_out[...] = new_a, a_one, a_two
        high, low = two_terms(new_a)
        none = jnp.zeros_like(high)
        first, second = attn[:HALF, :], attn[HALF:, :]
        two_in[...] = (
            dot_t(first, jnp.concatenate([high, none], axis=0))
            + dot_t(second, jnp.concatenate([none, high], axis=0))
        ) + (
            dot_t(first, jnp.concatenate([low, none], axis=0))
            + dot_t(second, jnp.concatenate([none, low], axis=0))
        )
        sum_two.one()
        new_b, b_one, b_two = apply_adam_step(
            b_ref[...], bm_ref[...], bv_ref[...], grad_out[RANK:, :]
        )
        b_out[...], bm_out[...], bv_out[...] = new_b, b_one, b_two

    ways = [at(lax.rem(z + 1, ZN), y, c), at(lax.rem(z + ZN - 1, ZN), y, c)]

    def product(u, other_y, other_c):
        yy = (1 - y) if other_y else y
        cc = (1 - c) if other_c else c
        to = lax.rem(z + ZN + 4 + (1 - 2 * lax.rem(u, 2)) * ((u + 1) // 2), ZN)
        block = (to * 2 + yy) * 2 + cc
        cols = pl.ds(pl.multiple_of(block * FEAT, FEAT), FEAT)
        return dot(attn[...], w[:, cols])

    def core_copy(u):
        return remote(csend.at[u], crecv.at[u], c_s.at[u], c_r.at[u], core_peer)

    def y_copy(u):
        return remote(ysend.at[u], yrecv.at[u], y_s.at[u], y_r.at[u], y_peer)

    def core_stage(u):
        for k in range(2):
            csend[u, k] = product(u, k == 1, True)
        core_copy(u).start()

    def y_stage(u):
        own = product(u, False, False)
        other = product(u, True, False)
        core_copy(u).wait_recv()
        own = own + crecv[u, 0]
        other = other + crecv[u, 1]
        for half in range(2):
            low, mid, high = half * HALF, half * HALF + FIRST, (half + 1) * HALF
            ysend[u, half] = other[mid:high]
            zs[u, half, STREAMS[0], :] = other[low:mid]
            zs[u, half, STREAMS[1], :] = own[low:mid]
            zs[u, half, STREAMS[2], :] = own[mid:high]

    def y_add(u):
        y_copy(u).wait_recv()
        for half in range(2):
            zs[u, half, STREAMS[2], :] += yrecv[u, half]

    def unit(step, way):
        return 0 if step == 0 else 2 * step - 1 + way

    def z_copy(step, way, half, stream):
        return remote(
            zs.at[unit(step, way), half, STREAMS[stream]],
            zr.at[step, way, half, STREAMS[stream]],
            z_s.at[step, way, half, stream],
            z_r.at[step, way, half, stream],
            ways[way],
        )

    def z_send(step, stream, late):
        for way in range(2):
            half = way if late else 1 - way
            if step > 0 and (late or step > 1):
                z_copy(step - 1, way, half, stream).wait_recv()
                rows = STREAMS[stream]
                zs[unit(step, way), half, rows, :] += zr[step - 1, way, half, rows, :]
            z_copy(step, way, half, stream).start()

    def z_end(stream):
        rows = STREAMS[stream]
        for half in range(2):
            for way in range(2):
                z_copy(3, way, half, stream).wait_recv()
            zs[7, half, rows, :] += zr[3, 0, half, rows, :] + zr[3, 1, half, rows, :]

    def rest():
        sum_one.finish()
        for k in range(1, DP):
            grad_scatter(k).wait_send()
            grad_gather(k).wait_send()
        b_high, b_low = two_terms(b_out[...])
        none = jnp.zeros_like(b_high)
        right[0] = jnp.concatenate([b_high, none, b_high, none, b_low, none], axis=0)
        right[1] = jnp.concatenate([none, b_high, none, b_high, none, b_low], axis=0)

    def base_sum():
        yfin_copy().wait_recv()
        for half in range(2):
            low, mid = half * HALF, half * HALF + FIRST
            base[pl.ds(low, FIRST), :] = zs[7, half, STREAMS[1], :] + yfin[half]
            base[pl.ds(mid, HALF - FIRST), :] = zs[7, half, STREAMS[2], :]

    def drain():
        yfin_copy().wait_send()
        for u in range(8):
            core_copy(u).wait_send()
            y_copy(u).wait_send()
        for way in range(2):
            for stream in range(3):
                z_copy(0, way, way, stream).wait_send()
                for after in range(1, 4):
                    for half in range(2):
                        z_copy(after, way, half, stream).wait_send()

    def yfin_copy():
        return remote(yfin_src, yfin, yf_s, yf_r, y_peer)

    attend = Attention(lengths, q, keys, values, fk, fv, attn, qs, sc, sn, mixed)
    for load in loads[4:8]:
        load.wait()
    sum_one.two()
    for load in loads[11:]:
        load.start()
    attend.scores()
    for load in loads[8:10]:
        load.wait()
    attend.mix()
    loads[10].wait()

    def next_units(u, carry):
        core_stage(u + 2)
        y_stage(u)
        return carry

    core_stage(0)
    core_stage(1)
    core_stage(2)
    y_stage(0)
    y_copy(0).start()
    z_send(0, 0, True)
    z_send(0, 1, True)
    sum_one.three()
    lax.fori_loop(1, 3, next_units, 0)
    y_copy(1).start()
    z_send(1, 0, False)
    z_send(1, 1, False)
    y_copy(2).start()
    y_add(0)
    z_send(0, 2, True)
    z_send(1, 0, True)
    z_send(1, 1, True)
    sum_one.four()
    gradients()
    lax.fori_loop(3, 5, next_units, 0)
    y_copy(3).start()
    y_copy(4).start()
    y_add(1)
    y_add(2)
    z_send(1, 2, False)
    z_send(1, 2, True)
    for load in loads[11:]:
        load.wait()
    z_send(2, 0, False)
    z_send(2, 1, False)
    z_send(2, 0, True)
    z_send(2, 1, True)
    gradient_sum()
    next_units(5, 0)
    y_copy(5).start()
    y_add(3)
    y_add(4)
    z_send(2, 2, False)
    z_send(2, 2, True)
    update()
    lax.fori_loop(6, 8, lambda u, carry: (y_stage(u), carry)[1], 0)
    y_copy(6).start()
    y_copy(7).start()
    sum_two.two()
    z_send(3, 0, False)
    z_send(3, 0, True)
    z_send(3, 1, False)
    z_send(3, 1, True)
    sum_two.three()
    z_end(0)
    for half in range(2):
        yfin_src[half] = zs[7, half, STREAMS[0], :]
    yfin_copy().start()
    y_add(5)
    y_add(6)
    z_send(3, 2, False)
    z_send(3, 2, True)
    rest()
    sum_two.four()
    z_end(1)
    y_add(7)
    z_end(2)
    base_sum()
    drain()
    sum_two.five()
    u_high, u_low = two_terms(two_out[...])
    left = jnp.concatenate([u_high, u_low, u_high], axis=1)
    for half in range(2):
        rows = pl.ds(half * HALF, HALF)
        dec[rows, :] = (base[rows, :] + adapter_scale * dot(left, right[half])).astype(BF16)
    sum_two.finish()


def step(*args):
    vmem = pl.BlockSpec(memory_space=pltpu.VMEM)
    factor = jax.ShapeDtypeStruct((RANK, FEAT), F32)
    dma = pltpu.SemaphoreType.DMA
    places = [pltpu.SMEM if arg.ndim == 1 else pltpu.VMEM for arg in args]
    small = [
        pltpu.VMEM((256, 128), F32),
        pltpu.VMEM((128, 128), F32),
        pltpu.VMEM((128, 128), F32),
        pltpu.VMEM((CHIPS - 1, 16, 128), F32),
        pltpu.VMEM((256, 128), F32),
    ]
    return pl.pallas_call(
        step_kernel,
        out_shape=(jax.ShapeDtypeStruct((ROWS, FEAT), BF16),) + (factor,) * 6,
        in_specs=[pl.BlockSpec(memory_space=pltpu.HBM)] * len(args),
        out_specs=(vmem,) * 7,
        scratch_shapes=[
            *[place(arg.shape, arg.dtype) for place, arg in zip(places, args)],
            pltpu.VMEM((ROWS, FEAT), BF16),
            pltpu.VMEM((ROWS, FEAT), F32),
            pltpu.VMEM((2, 6 * RANK, FEAT), BF16),
            pltpu.VMEM((512, 128), BF16),
            pltpu.VMEM((512, 256), F32),
            pltpu.VMEM((512, 128), F32),
            pltpu.VMEM((512, 128), F32),
            pltpu.VMEM((8, 2, ROWS, FEAT), F32),
            pltpu.VMEM((8, 2, ROWS, FEAT), F32),
            pltpu.VMEM((8, 2, HALF - FIRST, FEAT), F32),
            pltpu.VMEM((8, 2, HALF - FIRST, FEAT), F32),
            pltpu.VMEM((8, 2, HALF + FIRST, FEAT), F32),
            pltpu.VMEM((4, 2, 2, HALF + FIRST, FEAT), F32),
            pltpu.VMEM((2, FIRST, FEAT), F32),
            pltpu.VMEM((2, FIRST, FEAT), F32),
            *small,
            pltpu.VMEM((128, FEAT), F32),
            pltpu.VMEM((7, 16, FEAT), F32),
            pltpu.VMEM((128, FEAT), F32),
            pltpu.VMEM((128, 128), F32),
            pltpu.VMEM((64, 128), F32),
            pltpu.VMEM((64, 128), F32),
            pltpu.VMEM((CHIPS - 1, 8, 128), F32),
            pltpu.VMEM((128, 128), F32),
            dma((len(args),)),
            dma((8,)), dma((8,)), dma((8,)), dma((8,)),
            dma((4, 2, 2, 3)), dma((4, 2, 2, 3)),
            dma, dma,
            dma((78,)), dma((78,)),
        ],
        compiler_params=pltpu.CompilerParams(
            collective_id=0, has_side_effects=True, vmem_limit_bytes=52 * 1024 * 1024
        ),
    )(*[pltpu.with_memory_space_constraint(arg, pltpu.HBM) for arg in args])


def hand_out_kernel(*refs):
    half = len(refs) // 2
    copies = [
        pltpu.make_async_copy(src, dst, refs[-1].at[i])
        for i, (src, dst) in enumerate(zip(refs[:half], refs[half:-1]))
    ]
    for copy in copies:
        copy.start()
    for copy in copies:
        copy.wait()


def hand_out(*args):
    return pl.pallas_call(
        hand_out_kernel,
        out_shape=tuple(jax.ShapeDtypeStruct(arg.shape, arg.dtype) for arg in args),
        in_specs=[pl.BlockSpec(memory_space=pltpu.VMEM)] * len(args),
        out_specs=(pl.BlockSpec(memory_space=pltpu.HBM),) * len(args),
        scratch_shapes=[pltpu.SemaphoreType.DMA((len(args),))],
        compiler_params=pltpu.CompilerParams(vmem_limit_bytes=4 * 1024 * 1024),
    )(*args)


def per_device(
    projection_input,
    output_gradient,
    adapter_down,
    adapter_up,
    down_first_moment,
    down_second_moment,
    up_first_moment,
    up_second_moment,
    projection_weight,
    queries,
    stored_keys,
    stored_values,
    fresh_keys,
    fresh_values,
    lengths,
):
    results = step(
        projection_input,
        output_gradient,
        adapter_down.T,
        adapter_up,
        lengths,
        queries.reshape(ROWS, FEAT),
        fresh_keys.reshape(ROWS, 128),
        stored_keys,
        fresh_values.reshape(ROWS, 128),
        stored_values,
        projection_weight,
        down_first_moment.T,
        down_second_moment.T,
        up_first_moment,
        up_second_moment,
    )
    decoded, new_a, new_b, a_one, a_two, b_one, b_two = hand_out(*results)
    return (
        decoded.reshape(queries.shape), new_a.T, new_b, a_one.T, a_two.T, b_one, b_two
    )


def solution(mesh):
    return jax.shard_map(
        per_device,
        mesh=mesh,
        in_specs=(
            P("dp", "tensor"),
            P("dp", "tensor"),
            P("tensor", None),
            P(None, "tensor"),
            P("tensor", None),
            P("tensor", None),
            P(None, "tensor"),
            P(None, "tensor"),
            P("tensor", None),
            P(None, "dp", "tensor"),
            P("dp", None, "tensor"),
            P("dp", None, "tensor"),
            P(None, "dp", "tensor"),
            P(None, "dp", "tensor"),
            P("dp"),
        ),
        out_specs=(
            P(None, "dp", "tensor"),
            P("tensor", None),
            P(None, "tensor"),
            P("tensor", None),
            P("tensor", None),
            P(None, "tensor"),
            P(None, "tensor"),
        ),
        check_vma=False,
    )
```
